512 devices in a mesh: node: 64 (over z_hi, x, y), local: 8 (over z_lo, core).
Axes of the slice: x: 4, y: 8, z: 8 (z_hi: 2, z_lo: 4; z = z_hi * 4 + z_lo), core: 2. Of those that a mesh axis runs over, the one named last changes fastest.
Arguments:
- tokens: bfloat16 [2048, 8192], P('node', 'local'), may hold values from -6 to 6
- cotangent: bfloat16 [2048, 8192], P('node', 'local'), may hold values from -6 to 6
- gate_weight: bfloat16 [3584, 8192], P('node', 'local'), may hold values from -0.0625 to 0.0625
- up_weight: bfloat16 [3584, 8192], P('node', 'local'), may hold values from -0.0625 to 0.0625
- down_weight: bfloat16 [3584, 8192], P('node', 'local'), may hold values from -0.09375 to 0.09375
- gate_probe: bfloat16 [3584, 8192], P('node', 'local'), may hold values from -6 to 6
- up_probe: bfloat16 [3584, 8192], P('node', 'local'), may hold values from -6 to 6
Outputs:
- gate_diag: float32 [3584, 8192], P('node', 'local')
- up_diag: float32 [3584, 8192], P('node', 'local')
The draws below stay inside these ranges and needn't reach their ends.
All inputs are finite; a program needn't handle non-finite values.
Results may differ from the reference program's by a relative error of at most 0.0029.
Values may be sent and summed in bfloat16 or wider, within the bound.
No kernel may reach another device: no remote copies, remote signals or barrier semaphores. Data moves between devices by JAX's collectives and lax.ppermute only.
A program may use at most 64 MiB of HBM per device.

```python
import jax
import jax.numpy as jnp

D = 8192
F = 3584
TOKENS = 2048


def levels(key, shape, shards, smallest, largest):
    level, own = 1.0, jax.random.fold_in(key, 6)
    for dim, blocks in shards:
        draws = jnp.exp(jax.random.uniform(jax.random.fold_in(own, dim), (blocks,), jnp.float32, smallest / len(shards), largest / len(shards)))
        level = level * jnp.repeat(draws, shape[dim] // blocks).reshape([-1 if axis == dim else 1 for axis in range(len(shape))])
    return level


def bell_draw(stream_key, dims, spread, limit, split=(), kind=jnp.bfloat16):
    factor_of = levels(stream_key, dims, split, -0.22, 0.18) if split else 1.0
    entries = jax.random.normal(stream_key, dims, jnp.float32) * spread * factor_of
    return jnp.minimum(jnp.maximum(entries, -limit), limit).astype(kind)


def setup_inputs(seed: int = 0) -> dict:
    key_of = jax.random.split(jax.random.key(seed), 8)
    tokens = bell_draw(key_of[0], (TOKENS, D), 1.0, 6.0, ((0, 64), (1, 8)))
    cotangent = bell_draw(key_of[1], (TOKENS, D), 1.0, 6.0, ((0, 64), (1, 8)))
    gate_weight = bell_draw(key_of[2], (F, D), D ** -0.5, 0.0625, ((0, 64), (1, 8)))
    up_weight = bell_draw(key_of[3], (F, D), D ** -0.5, 0.0625, ((0, 64), (1, 8)))
    down_weight = bell_draw(key_of[4], (F, D), F ** -0.5, 0.09375, ((0, 64), (1, 8)))
    gate_probe = bell_draw(key_of[5], (F, D), 1.0, 6.0, ((0, 64), (1, 8)))
    up_probe = bell_draw(key_of[6], (F, D), 1.0, 6.0, ((0, 64), (1, 8)))
    return {"tokens": tokens, "cotangent": cotangent, "gate_weight": gate_weight, "up_weight": up_weight, "down_weight": down_weight, "gate_probe": gate_probe, "up_probe": up_probe}


def project(rows, weight):
    return jnp.dot(rows, weight.T, preferred_element_type=jnp.float32)


def reference(tokens, cotangent, gate_weight, up_weight, down_weight, gate_probe, up_probe):
    pre_gate = project(tokens, gate_weight)
    pre_up = project(tokens, up_weight)
    tan_gate = project(tokens, gate_probe)
    tan_up = project(tokens, up_probe)
    back = project(cotangent, down_weight)
    sig = jax.nn.sigmoid(pre_gate)
    slope = sig * (1.0 + pre_gate * (1.0 - sig))
    bend = sig * (1.0 - sig) * (2.0 + pre_gate * (1.0 - 2.0 * sig))
    fac_gate = (back * (tan_up * slope + pre_up * bend * tan_gate)).astype(jnp.bfloat16)
    fac_up = (back * slope * tan_gate).astype(jnp.bfloat16)
    hvp_gate = jnp.dot(fac_gate.T, tokens, preferred_element_type=jnp.float32) / TOKENS
    hvp_up = jnp.dot(fac_up.T, tokens, preferred_element_type=jnp.float32) / TOKENS
    gate_diag = gate_probe.astype(jnp.float32) * hvp_gate
    up_diag = up_probe.astype(jnp.float32) * hvp_up
    return gate_diag, up_diag
```

```python
import jax
import jax.numpy as jnp
from jax import lax
from jax.sharding import Mesh, PartitionSpec as P

NODE = {"zh": 2, "x": 4, "y": 8}
LOCAL = {"zl": 4, "c": 2}

PRE_SCALE = 64.0
TAN_SCALE = 0.5
BACK_SCALE = 32.0


def swap(value, axis):
    return lax.ppermute(value, axis, [(0, 1), (1, 0)])


def shift(value, axis, by):
    size = lax.axis_size(axis)
    return lax.ppermute(value, axis, [(i, (i + by) % size) for i in range(size)])


def ring_blocks(block, axis):
    size = lax.axis_size(axis)
    half = block.shape[0] // 2
    ahead = behind = block
    blocks = [block]
    for _ in range(size // 2 - 1):
        ahead, behind = shift(ahead, axis, 1), shift(behind, axis, -1)
        blocks += [ahead, behind]
    far = (shift(ahead[:half], axis, 1), shift(behind[half:], axis, -1))
    blocks.append(jnp.concatenate(far, axis=0))
    return blocks


def project(rows, weight):
    return lax.dot_general(
        rows, weight, (((1,), (1,)), ((), ())), preferred_element_type=jnp.float32
    )


def factors(pre_gate, pre_up, tan_gate, tan_up, back):
    sig = jax.nn.sigmoid(pre_gate)
    slope = sig * (1.0 + pre_gate * (1.0 - sig))
    bend = sig * (1.0 - sig) * (2.0 + pre_gate * (1.0 - 2.0 * sig))
    fac_gate = (back * (tan_up * slope + pre_up * bend * tan_gate)).astype(jnp.bfloat16)
    fac_up = (back * slope * tan_gate).astype(jnp.bfloat16)
    return (fac_gate, fac_up)


def on_device(tokens, cotangent, gate_weight, up_weight, down_weight, gate_probe, up_probe):
    nx, nzl, nc = lax.axis_size("x"), lax.axis_size("zl"), lax.axis_size("c")
    own, feats = tokens.shape
    hid = gate_weight.shape[0]
    total = own * lax.axis_size(("zh", "x", "y"))
    core = lax.axis_index("c")

    mats = jnp.concatenate([gate_weight, up_weight, gate_probe, up_probe, down_weight], axis=0)
    mats = lax.all_gather(mats, "x", axis=0, tiled=False)
    mats = mats.reshape(nx, 5, hid, feats).transpose(1, 0, 2, 3).reshape(5 * nx * hid, feats)
    w_tok, w_cot = mats[: 4 * nx * hid], mats[4 * nx * hid :]

    rows = jnp.concatenate([tokens, cotangent], axis=0)
    rows = jnp.stack([rows, swap(rows, "zh")], axis=0)
    blocks = ring_blocks(rows, "y")
    x_rows = jnp.concatenate([b[:, :own] for b in blocks], axis=0).reshape(-1, feats)
    g_rows = jnp.concatenate([b[:, own:] for b in blocks], axis=0).reshape(-1, feats)
    x_all = lax.all_gather(x_rows, "x", axis=0, tiled=True)

    count = x_rows.shape[0] // nc
    def term(which):
        x_half = lax.dynamic_slice_in_dim(x_rows, which * count, count, 0)
        g_half = lax.dynamic_slice_in_dim(g_rows, which * count, count, 0)
        return jnp.concatenate([project(x_half, w_tok), project(g_half, w_cot)], axis=1)
    other = swap(term(1 - core), "c")
    terms = term(core) + other

    width = nx * hid
    scale = jnp.repeat(
        jnp.array([PRE_SCALE, PRE_SCALE, TAN_SCALE, TAN_SCALE, BACK_SCALE], jnp.float32), width
    )[None, :]
    sent = (terms * scale).astype(jnp.float16)
    got = lax.all_to_all(sent.reshape(nzl, count // nzl, 5 * width), "zl", 0, 0, tiled=True)
    proj = jnp.sum(got.astype(jnp.float32), axis=0) * (1.0 / scale)
    parts = [proj[:, i * width : (i + 1) * width] for i in range(5)]
    fac_gate, fac_up = factors(*parts)

    share = count // nzl
    fac = jnp.stack([fac_gate, fac_up], axis=1).reshape(share, 2, nx, hid)
    fac = fac.transpose(2, 0, 1, 3).reshape(nx, 1, share, 2 * hid)
    fac = jnp.broadcast_to(fac, (nx, nzl, share, 2 * hid)).reshape(nx * nzl, share, 2 * hid)
    fac = lax.all_to_all(fac, ("x", "zl"), 0, 0, tiled=True)
    fac = fac.reshape(nx, 1, count, 2 * hid)
    fac_other = swap(fac, "c")
    fac = jnp.where(
        core == 0,
        jnp.concatenate([fac, fac_other], axis=1),
        jnp.concatenate([fac_other, fac], axis=1),
    ).reshape(-1, 2 * hid)

    hvp = lax.dot_general(
        fac, x_all, (((0,), (0,)), ((), ())), preferred_element_type=jnp.float32
    ) / total
    gate_diag = gate_probe.astype(jnp.float32) * hvp[:hid]
    up_diag = up_probe.astype(jnp.float32) * hvp[hid:]
    return (gate_diag, up_diag)


def solution(mesh):
    sizes = {**NODE, **LOCAL}
    cut = Mesh(mesh.devices.reshape(tuple(sizes.values())), tuple(sizes))
    placed = P(tuple(NODE), tuple(LOCAL))
    return jax.shard_map(
        on_device,
        mesh=cut,
        in_specs=(placed,) * 7,
        out_specs=(placed, placed),
        check_vma=False,
    )
```

```python
import jax
import jax.numpy as jnp
from jax import lax
from jax.sharding import Mesh, PartitionSpec as P

NODE = {"zh": 2, "x": 4, "y": 8}
LOCAL = {"zl": 4, "c": 2}

PRE_SCALE = 64.0
TAN_SCALE = 0.5
BACK_SCALE = 32.0

SHIFTS = (1, -1, 2)


def swap(value, axis):
    return lax.ppermute(value, axis, [(0, 1), (1, 0)])


def shift(value, axis, by):
    size = lax.axis_size(axis)
    return lax.ppermute(value, axis, [(i, (i + by) % size) for i in range(size)])


def ring_step(value):
    size = lax.axis_size("y")
    pairs = []
    for y in range(size):
        pairs.append((2 * y, 2 * ((y + 1) % size)))
        pairs.append((2 * y + 1, 2 * ((y - 1) % size) + 1))
    return lax.ppermute(value, ("y", "c"), pairs)


def contract(left, right, dims):
    return lax.dot_general(left, right, (dims, ((), ())), preferred_element_type=jnp.float32)


def factors(pre_gate, pre_up, tan_gate, tan_up, back):
    sig = jax.nn.sigmoid(pre_gate)
    slope = sig * (1.0 + pre_gate * (1.0 - sig))
    bend = sig * (1.0 - sig) * (2.0 + pre_gate * (1.0 - 2.0 * sig))
    fac_gate = (back * (tan_up * slope + pre_up * bend * tan_gate)).astype(jnp.bfloat16)
    fac_up = (back * slope * tan_gate).astype(jnp.bfloat16)
    return (fac_gate, fac_up)


def on_device(tokens, cotangent, gate_weight, up_weight, down_weight, gate_probe, up_probe):
    nx, ny, nzl = lax.axis_size("x"), lax.axis_size("y"), lax.axis_size("zl")
    own, feats = tokens.shape
    hid = gate_weight.shape[0]
    total = own * lax.axis_size(("zh", "x", "y"))
    x, core = lax.axis_index("x"), lax.axis_index("c")

    rows = jnp.concatenate([tokens, cotangent], axis=0)
    rows = jnp.stack([rows, swap(rows, "zh")], axis=0)
    others = swap(rows, "c")
    tok = jnp.stack([rows[:, :own], others[:, :own]], axis=0)
    cot = jnp.stack([rows[:, own:], others[:, own:]], axis=0)

    tall = -(-hid // 16) * 16
    fill = jnp.zeros((tall - hid, feats), jnp.bfloat16)
    mats = jnp.concatenate(
        [gate_weight, up_weight, gate_probe, up_probe, down_weight, fill], axis=0
    )
    width = mats.shape[0]
    w_own = jnp.zeros((nx, width, feats), jnp.bfloat16)
    w_own = lax.dynamic_update_index_in_dim(w_own, mats, x, 0)
    for by in SHIFTS:
        w_own = lax.dynamic_update_index_in_dim(
            w_own, shift(mats, "x", by), (x - by) % nx, 0
        )
    w_other = swap(w_own, "c")

    def half(block):
        return lax.dynamic_slice_in_dim(block, core, 1, 1)
    toks, cots = [half(tok)], [half(cot)]
    for _ in range(ny // 2 - 1):
        tok, cot = ring_step(tok), ring_step(cot)
        toks.append(tok)
        cots.append(cot)
    toks.append(ring_step(half(tok)))
    cots.append(ring_step(half(cot)))
    toks = jnp.concatenate(toks, axis=1).reshape(2, -1, feats)
    cots = jnp.concatenate(cots, axis=1).reshape(2, -1, feats)
    count = toks.shape[1]
    toks_x = [toks] + [shift(toks, "x", by) for by in SHIFTS]

    w_own, w_other = w_own.reshape(nx * width, feats), w_other.reshape(nx * width, feats)
    def term(block):
        return contract(block[0], w_own, ((1,), (1,))) + contract(block[1], w_other, ((1,), (1,)))
    column = lax.broadcasted_iota(jnp.int32, (1, nx * width), 1) % width
    terms = jnp.where(column >= 4 * hid, term(cots), term(toks))
    scale = jnp.where(
        column >= 4 * hid, BACK_SCALE, jnp.where(column >= 2 * hid, TAN_SCALE, PRE_SCALE)
    )
    share = count // nzl
    sent = (terms * scale).astype(jnp.float16).reshape(nzl, share, nx * width)
    got = lax.all_to_all(sent, "zl", 0, 0, tiled=True)
    proj = jnp.sum(got.astype(jnp.float32), axis=0) * (1.0 / scale)
    proj = proj.reshape(share, nx, width)
    parts = [proj[:, :, i * hid : (i + 1) * hid] for i in range(5)]
    fac = jnp.concatenate(factors(*parts), axis=2)

    fac = fac.transpose(1, 0, 2).reshape(nx, 1, share, 2 * hid)
    fac = jnp.broadcast_to(fac, (nx, nzl, share, 2 * hid)).reshape(nx * nzl, share, 2 * hid)
    fac = lax.all_to_all(fac, ("x", "zl"), 0, 0, tiled=True)
    fac = fac.reshape(nx, count, 2 * hid)

    facs = [lax.dynamic_index_in_dim(fac, (x - by) % nx, 0, False) for by in (0,) + SHIFTS]
    def hvp(which):
        return sum(contract(f, t[which], ((0,), (0,))) for f, t in zip(facs, toks_x))
    other = swap(hvp(1), "c")
    both = (hvp(0) + other) / total
    gate_diag = gate_probe.astype(jnp.float32) * both[:hid]
    up_diag = up_probe.astype(jnp.float32) * both[hid:]
    return (gate_diag, up_diag)


def solution(mesh):
    sizes = {**NODE, **LOCAL}
    cut = Mesh(mesh.devices.reshape(tuple(sizes.values())), tuple(sizes))
    placed = P(tuple(NODE), tuple(LOCAL))
    return jax.shard_map(
        on_device,
        mesh=cut,
        in_specs=(placed,) * 7,
        out_specs=(placed, placed),
        check_vma=False,
    )
```

```python
import functools

import jax
import jax.numpy as jnp
from jax import lax
from jax.experimental import pallas as pl
from jax.experimental.pallas import tpu as pltpu
from jax.sharding import Mesh, PartitionSpec as P

NODE = {"zh": 2, "x": 4, "y": 8}
LOCAL = {"zl": 4, "c": 2}

PRE_SCALE = 64.0
TAN_SCALE = 0.5
BACK_SCALE = 32.0

VMEM = pl.BlockSpec(memory_space=pltpu.VMEM)
SMEM = pl.BlockSpec(memory_space=pltpu.SMEM)


def swap(value, axis):
    return lax.ppermute(value, axis, [(0, 1), (1, 0)])


def shift(value, axis, by):
    size = lax.axis_size(axis)
    return lax.ppermute(value, axis, [(i, (i + by) % size) for i in range(size)])


def local_call(body, out_shape, scratch, flops, moved, interpret, *args):
    return pl.pallas_call(
        body,
        out_shape=out_shape,
        in_specs=[SMEM] + [VMEM] * (len(args) - 1),
        out_specs=jax.tree.map(lambda _: VMEM, out_shape),
        scratch_shapes=scratch,
        cost_estimate=pl.CostEstimate(flops=flops, bytes_accessed=moved, transcendentals=0),
        compiler_params=pltpu.CompilerParams(vmem_limit_bytes=24 * 1024 * 1024),
        interpret=interpret,
    )(*args)


def terms_kernel(own, place, *refs):
    *refs, out, x_half, g_half, w_all = refs
    blocks, weights = refs[:-4], refs[-4:]
    middle = len(blocks) // 2
    tall = weights[0].shape[0]
    tok_rows = tall * 7 // 9
    cot_rows = tall - tok_rows
    for i, weight in enumerate(weights):
        w_all[i * tok_rows : (i + 1) * tok_rows] = weight[:tok_rows]
        start = 4 * tok_rows + i * cot_rows
        w_all[start : start + cot_rows] = weight[tok_rows:]

    def take(chosen):
        row = 0
        for block in chosen:
            for z in range(block.shape[0]):
                x_half[row : row + own] = block[z, :own]
                g_half[row : row + own] = block[z, own:]
                row += own

    @pl.when(place[0] == 0)
    def _():
        take(blocks[:middle])

    @pl.when(place[0] != 0)
    def _():
        take(blocks[middle:])

    across = (((1,), (1,)), ((), ()))
    cut = 4 * tok_rows
    out[:, :cut] = lax.dot_general(
        x_half[...], w_all[:cut], across, preferred_element_type=jnp.float32
    )
    out[:, cut:] = lax.dot_general(
        g_half[...], w_all[cut:], across, preferred_element_type=jnp.float32
    )


def hvp_kernel(total, place, mine, other, *refs):
    *tokens, gate_probe, up_probe, gate_diag, up_diag = refs
    x, core = place[0], place[1]
    sizes = len(tokens) // 4
    acc = None
    for by in range(4):
        source = lax.rem(x - by + 4, 4)
        first, second = mine[source], other[source]
        fac = jnp.concatenate(
            [jnp.where(core == 0, first, second), jnp.where(core == 0, second, first)], axis=0
        )
        row = 0
        for part in tokens[by * sizes : (by + 1) * sizes]:
            rows = part.shape[0]
            term = lax.dot_general(
                fac[row : row + rows], part[...], (((0,), (0,)), ((), ())),
                preferred_element_type=jnp.float32,
            )
            acc = term if acc is None else acc + term
            row += rows
    acc = acc / total
    hid = gate_diag.shape[0]
    gate_diag[...] = gate_probe[...].astype(jnp.float32) * acc[:hid]
    up_diag[...] = up_probe[...].astype(jnp.float32) * acc[hid:]


def factors(pre_gate, pre_up, tan_gate, tan_up, back):
    sig = jax.nn.sigmoid(pre_gate)
    slope = sig * (1.0 + pre_gate * (1.0 - sig))
    bend = sig * (1.0 - sig) * (2.0 + pre_gate * (1.0 - 2.0 * sig))
    fac_gate = (back * (tan_up * slope + pre_up * bend * tan_gate)).astype(jnp.bfloat16)
    fac_up = (back * slope * tan_gate).astype(jnp.bfloat16)
    return (fac_gate, fac_up)


def stacked(parts, rows):
    row, out = 0, None
    for part in parts:
        padded = lax.pad(
            part, jnp.zeros((), part.dtype),
            ((row, rows - row - part.shape[0], 0), (0, 0, 0)),
        )
        out = padded if out is None else out + padded
        row += part.shape[0]
    return out


def on_device(
    tokens, cotangent, gate_weight, up_weight, down_weight, gate_probe, up_probe, interpret
):
    nx, ny, nzl = lax.axis_size("x"), lax.axis_size("y"), lax.axis_size("zl")
    own, feats = tokens.shape
    hid = gate_weight.shape[0]
    total = own * lax.axis_size(("zh", "x", "y"))
    x, core = lax.axis_index("x"), lax.axis_index("c")

    rows = stacked([tokens, cotangent], 2 * own)
    block = jnp.stack([rows, swap(rows, "zh")], axis=0)

    tok_rows, cot_rows = 4 * hid, hid * 8 // 7
    mats = stacked(
        [gate_weight, up_weight, gate_probe, up_probe, down_weight], tok_rows + cot_rows
    )
    weights = [mats] + [shift(mats, "x", by) for by in (1, 2, -1)]

    ahead = behind = block
    blocks = [block]
    for _ in range(ny // 2 - 1):
        ahead, behind = shift(ahead, "y", 1), shift(behind, "y", -1)
        blocks += [ahead, behind]
    far = (shift(ahead[:1], "y", 1), shift(behind[1:], "y", -1))
    blocks.append(jnp.concatenate(far, axis=0))

    near = len(blocks) - 3
    chunks = []
    for part in (blocks[:near], blocks[near:]):
        part = jnp.concatenate([b[:, :own] for b in part], axis=0).reshape(-1, feats)
        chunks.append([part] + [shift(part, "x", by) for by in (1, 2, -1)])

    count = len(blocks) * own
    columns = nx * (tok_rows + cot_rows)
    term = functools.partial(
        local_call,
        functools.partial(terms_kernel, own),
        jax.ShapeDtypeStruct((count, columns), jnp.float32),
        [
            pltpu.VMEM((count, feats), jnp.bfloat16),
            pltpu.VMEM((count, feats), jnp.bfloat16),
            pltpu.VMEM((columns, feats), jnp.bfloat16),
        ],
        2 * count * columns * feats,
        2 * columns * feats,
        interpret,
    )
    other = swap(term((1 - core).reshape(1), *blocks, *weights), "c")
    terms = term(core.reshape(1), *blocks, *weights) + other

    column = lax.broadcasted_iota(jnp.int32, (1, columns), 1)
    scale = jnp.where(
        column >= nx * tok_rows,
        BACK_SCALE,
        jnp.where(column % tok_rows >= 2 * hid, TAN_SCALE, PRE_SCALE),
    )
    share = count // nzl
    sent = (terms * scale).astype(jnp.float16).reshape(nzl, share, columns)
    got = lax.all_to_all(sent, "zl", 0, 0, tiled=True)
    proj = jnp.sum(got.astype(jnp.float32), axis=0) * (1.0 / scale)
    tok_part = proj[:, : nx * tok_rows].reshape(share, nx, 4, hid)
    back = proj[:, nx * tok_rows :].reshape(share, nx, cot_rows)[:, :, :hid]
    fac = jnp.concatenate(factors(*[tok_part[:, :, i] for i in range(4)], back), axis=2)

    fac = fac.transpose(1, 0, 2)
    fac = jnp.stack(
        [lax.dynamic_index_in_dim(fac, (x - i) % nx, 0, False) for i in range(nx)], axis=0
    ).reshape(nx, 1, share, 2 * hid)
    fac = jnp.broadcast_to(fac, (nx, nzl, share, 2 * hid)).reshape(nx * nzl, share, 2 * hid)
    fac = lax.all_to_all(fac, ("x", "zl"), 0, 0, tiled=True).reshape(nx, count, 2 * hid)
    fac_other = swap(fac, "c")

    diag = jax.ShapeDtypeStruct((hid, feats), jnp.float32)
    return local_call(
        functools.partial(hvp_kernel, total),
        (diag, diag),
        [],
        4 * hid * total * feats,
        2 * total * feats,
        interpret,
        jnp.stack([x, core]),
        fac,
        fac_other,
        *[chunk[by] for by in range(nx) for chunk in chunks],
        gate_probe,
        up_probe,
    )


def solution(mesh, interpret=False):
    sizes = {**NODE, **LOCAL}
    cut = Mesh(mesh.devices.reshape(tuple(sizes.values())), tuple(sizes))
    placed = P(tuple(NODE), tuple(LOCAL))
    return jax.shard_map(
        functools.partial(on_device, interpret=interpret),
        mesh=cut,
        in_specs=(placed,) * 7,
        out_specs=(placed, placed),
        check_vma=False,
    )
```

```python
import functools

import jax
import jax.numpy as jnp
from jax import lax
from jax.experimental import pallas as pl
from jax.experimental.pallas import tpu as pltpu
from jax.sharding import Mesh, PartitionSpec as P

NODE = {"zh": 2, "x": 4, "y": 8}
LOCAL = {"zl": 4, "c": 2}

PRE_SCALE = 64.0
TAN_SCALE = 0.5
BACK_SCALE = 32.0

VMEM = pl.BlockSpec(memory_space=pltpu.VMEM)
SMEM = pl.BlockSpec(memory_space=pltpu.SMEM)


def swap(value, axis):
    return lax.ppermute(value, axis, [(0, 1), (1, 0)])


def shift(value, axis, by):
    size = lax.axis_size(axis)
    return lax.ppermute(value, axis, [(i, (i + by) % size) for i in range(size)])


def local_call(body, out_shape, flops, moved, interpret, *args, **options):
    return pl.pallas_call(
        body,
        out_shape=out_shape,
        cost_estimate=pl.CostEstimate(flops=flops, bytes_accessed=moved, transcendentals=0),
        compiler_params=pltpu.CompilerParams(vmem_limit_bytes=12 * 1024 * 1024),
        interpret=interpret,
        **options,
    )(*args)


def reorder_kernel(tok_rows, gathered, out):
    nx, rows, _ = gathered.shape
    cot_rows = rows - tok_rows
    for i in range(nx):
        out[i * tok_rows : (i + 1) * tok_rows] = gathered[i, :tok_rows]
        start = nx * tok_rows + i * cot_rows
        out[start : start + cot_rows] = gathered[i, tok_rows:]


def terms_kernel(own, cut, place, *refs):
    *blocks, weights, out, x_half, g_half = refs
    slabs = [(block, z) for block in blocks for z in range(block.shape[0])]
    middle = len(slabs) // 2

    def take(chosen):
        for i, (block, z) in enumerate(chosen):
            x_half[i * own : (i + 1) * own] = block[z, :own]
            g_half[i * own : (i + 1) * own] = block[z, own:]

    @pl.when(place[0] == 0)
    def _():
        take(slabs[:middle])

    @pl.when(place[0] != 0)
    def _():
        take(slabs[middle:])

    across = (((1,), (1,)), ((), ()))
    out[:, :cut] = lax.dot_general(
        x_half[...], weights[:cut], across, preferred_element_type=jnp.float32
    )
    out[:, cut:] = lax.dot_general(
        g_half[...], weights[cut:], across, preferred_element_type=jnp.float32
    )


def hvp_kernel(total, place, mine, other, *refs):
    *tokens, gate_probe, up_probe, gate_diag, up_diag, acc = refs
    first, second = mine[0], other[0]
    fac = jnp.concatenate(
        [jnp.where(place[0] == 0, first, second), jnp.where(place[0] == 0, second, first)],
        axis=0,
    )
    term, row = None, 0
    for part in tokens:
        rows = part.shape[0]
        piece = lax.dot_general(
            fac[row : row + rows], part[...], (((0,), (0,)), ((), ())),
            preferred_element_type=jnp.float32,
        )
        term = piece if term is None else term + piece
        row += rows

    @pl.when(pl.program_id(0) == 0)
    def _():
        acc[...] = term

    @pl.when(pl.program_id(0) != 0)
    def _():
        acc[...] += term

    @pl.when(pl.program_id(0) == pl.num_programs(0) - 1)
    def _():
        hid = gate_diag.shape[0]
        gate_diag[...] = gate_probe[...].astype(jnp.float32) * (acc[:hid] / total)
        up_diag[...] = up_probe[...].astype(jnp.float32) * (acc[hid:] / total)


def factors(pre_gate, pre_up, tan_gate, tan_up, back):
    sig = jax.nn.sigmoid(pre_gate)
    slope = sig * (1.0 + pre_gate * (1.0 - sig))
    bend = sig * (1.0 - sig) * (2.0 + pre_gate * (1.0 - 2.0 * sig))
    fac_gate = (back * (tan_up * slope + pre_up * bend * tan_gate)).astype(jnp.bfloat16)
    fac_up = (back * slope * tan_gate).astype(jnp.bfloat16)
    return (fac_gate, fac_up)


def stacked(parts, rows):
    row, out = 0, None
    for part in parts:
        padded = lax.pad(
            part, jnp.zeros((), part.dtype),
            ((row, rows - row - part.shape[0], 0), (0, 0, 0)),
        )
        out = padded if out is None else out + padded
        row += part.shape[0]
    return out


def on_device(
    tokens, cotangent, gate_weight, up_weight, down_weight, gate_probe, up_probe, interpret
):
    nx, ny, nzl = lax.axis_size("x"), lax.axis_size("y"), lax.axis_size("zl")
    own, feats = tokens.shape
    hid = gate_weight.shape[0]
    total = own * lax.axis_size(("zh", "x", "y"))
    core = lax.axis_index("c")

    rows = stacked([tokens, cotangent], 2 * own)
    block = jnp.stack([rows, swap(rows, "zh")], axis=0)

    tok_rows, cot_rows = 4 * hid, hid * 8 // 7
    mats = stacked(
        [gate_weight, up_weight, gate_probe, up_probe, down_weight], tok_rows + cot_rows
    )
    mats = lax.all_gather(mats, "x", axis=0, tiled=False)
    cut, columns = nx * tok_rows, nx * (tok_rows + cot_rows)
    weights = local_call(
        functools.partial(reorder_kernel, tok_rows),
        jax.ShapeDtypeStruct((columns, feats), jnp.bfloat16),
        0, 4 * columns * feats, interpret, mats, in_specs=[VMEM], out_specs=VMEM,
    )

    ahead = behind = block
    blocks = [block]
    for _ in range(ny // 2 - 1):
        ahead, behind = shift(ahead, "y", 1), shift(behind, "y", -1)
        blocks += [ahead, behind]
    near = len(blocks) - 2
    blocks += [shift(ahead[:1], "y", 1), shift(behind[1:], "y", -1)]

    chunks = []
    for part in (blocks[:near], blocks[near:]):
        part = jnp.concatenate([b[:, :own] for b in part], axis=0).reshape(-1, feats)
        chunks.append(lax.all_gather(part, "x", axis=0, tiled=True))

    count = ny * own
    term = functools.partial(
        local_call,
        functools.partial(terms_kernel, own, cut),
        jax.ShapeDtypeStruct((count, columns), jnp.float32),
        2 * count * columns * feats,
        2 * columns * feats,
        interpret,
        in_specs=[SMEM] + [VMEM] * (len(blocks) + 1),
        out_specs=VMEM,
        scratch_shapes=[pltpu.VMEM((count, feats), jnp.bfloat16)] * 2,
    )
    other = swap(term((1 - core).reshape(1), *blocks, weights), "c")
    terms = term(core.reshape(1), *blocks, weights) + other

    column = lax.broadcasted_iota(jnp.int32, (1, columns), 1)
    scale = jnp.where(
        column >= nx * tok_rows,
        BACK_SCALE,
        jnp.where(column % tok_rows >= 2 * hid, TAN_SCALE, PRE_SCALE),
    )
    share = count // nzl
    sent = (terms * scale).astype(jnp.float16).reshape(nzl, share, columns)
    got = lax.all_to_all(sent, "zl", 0, 0, tiled=True)
    proj = jnp.sum(got.astype(jnp.float32), axis=0) * (1.0 / scale)
    tok_part = proj[:, : nx * tok_rows].reshape(share, nx, 4, hid)
    back = proj[:, nx * tok_rows :].reshape(share, nx, cot_rows)[:, :, :hid]
    fac = jnp.concatenate(factors(*[tok_part[:, :, i] for i in range(4)], back), axis=2)

    fac = fac.transpose(1, 0, 2).reshape(nx, 1, share, 2 * hid)
    fac = jnp.broadcast_to(fac, (nx, nzl, share, 2 * hid)).reshape(nx * nzl, share, 2 * hid)
    fac = lax.all_to_all(fac, ("x", "zl"), 0, 0, tiled=True).reshape(nx, count, 2 * hid)
    fac_other = swap(fac, "c")

    def whole(shape):
        return pl.BlockSpec(shape, lambda i: (0,) * len(shape))
    by_x = pl.BlockSpec((1, count, 2 * hid), lambda i: (i, 0, 0))
    diag = jax.ShapeDtypeStruct((hid, feats), jnp.float32)
    return local_call(
        functools.partial(hvp_kernel, total),
        (diag, diag),
        4 * hid * total * feats,
        2 * total * feats,
        interpret,
        core.reshape(1),
        fac,
        fac_other,
        *chunks,
        gate_probe,
        up_probe,
        grid=(nx,),
        in_specs=[SMEM, by_x, by_x]
        + [pl.BlockSpec((chunk.shape[0] // nx, feats), lambda i: (i, 0)) for chunk in chunks]
        + [whole(gate_probe.shape)] * 2,
        out_specs=(whole(diag.shape),) * 2,
        scratch_shapes=[pltpu.VMEM((2 * hid, feats), jnp.float32)],
    )


def solution(mesh, interpret=False):
    sizes = {**NODE, **LOCAL}
    cut = Mesh(mesh.devices.reshape(tuple(sizes.values())), tuple(sizes))
    placed = P(tuple(NODE), tuple(LOCAL))
    return jax.shard_map(
        functools.partial(on_device, interpret=interpret),
        mesh=cut,
        in_specs=(placed,) * 7,
        out_specs=(placed, placed),
        check_vma=False,
    )
```

```python
import functools

import jax
import jax.numpy as jnp
import numpy as np
from jax import lax
from jax.experimental import pallas as pl
from jax.experimental.pallas import tpu as pltpu
from jax.sharding import Mesh, PartitionSpec as P

NODE = {"zh": 2, "x": 4, "y": 8}
LOCAL = {"zl": 4, "c": 2}

PRE_SCALE = 64.0
TAN_SCALE = 0.5
BACK_SCALE = 32.0

VMEM = pl.BlockSpec(memory_space=pltpu.VMEM)
ANY = pl.BlockSpec(memory_space=pl.ANY)
SMEM = pl.BlockSpec(memory_space=pltpu.SMEM)


def swap(value, axis):
    return lax.ppermute(value, axis, [(0, 1), (1, 0)])


def shift(value, axis, by):
    size = lax.axis_size(axis)
    return lax.ppermute(value, axis, [(i, (i + by) % size) for i in range(size)])


def mix(value, axis, by):
    return lax.ppermute(value, axis, [(i, i ^ by) for i in range(lax.axis_size(axis))])


def local_call(body, out_shape, flops, moved, interpret, *args, **options):
    return pl.pallas_call(
        body,
        out_shape=out_shape,
        cost_estimate=pl.CostEstimate(flops=flops, bytes_accessed=moved, transcendentals=0),
        compiler_params=pltpu.CompilerParams(vmem_limit_bytes=16 * 1024 * 1024),
        interpret=interpret,
        **options,
    )(*args)


def terms_kernel(own, tok_rows, place, *refs):
    *blocks, out, x_half, g_half, w_all, row_sems, w_sems = refs
    blocks, weights = blocks[:-4], blocks[-4:]
    slabs = [(block, z) for block in blocks for z in range(block.shape[0])]
    middle = len(slabs) // 2
    cut = 4 * tok_rows
    cot_rows = weights[0].shape[0] - tok_rows

    copies = []
    for i, weight in enumerate(weights):
        tops = w_all.at[pl.ds(i * tok_rows, tok_rows)]
        rest = w_all.at[pl.ds(cut + i * cot_rows, cot_rows)]
        copies.append(
            pltpu.make_async_copy(weight.at[pl.ds(0, tok_rows)], tops, w_sems.at[2 * i])
        )
        copies.append(
            pltpu.make_async_copy(
                weight.at[pl.ds(tok_rows, cot_rows)], rest, w_sems.at[2 * i + 1]
            )
        )
    for copy in copies:
        copy.start()

    def take(chosen):
        moves = []
        for i, (block, z) in enumerate(chosen):
            row = pl.multiple_of((((i // 2) ^ place[1]) * 2 + i % 2) * own, own)
            for j, half in enumerate((x_half, g_half)):
                moves.append(
                    pltpu.make_async_copy(
                        block.at[z, pl.ds(j * own, own)],
                        half.at[pl.ds(row, own)],
                        row_sems.at[2 * i + j],
                    )
                )
        for move in moves:
            move.start()
        for move in moves:
            move.wait()

    @pl.when(place[0] == 0)
    def _():
        take(slabs[:middle])

    @pl.when(place[0] != 0)
    def _():
        take(slabs[middle:])

    for copy in copies:
        copy.wait()
    across = (((1,), (1,)), ((), ()))
    out[:, :cut] = lax.dot_general(
        x_half[...], w_all[:cut], across, preferred_element_type=jnp.float32
    )
    out[:, cut:] = lax.dot_general(
        g_half[...], w_all[cut:], across, preferred_element_type=jnp.float32
    )


def hvp_kernel(first, mine, other, kept, given, *outs):
    down = (((0,), (0,)), ((), ()))
    for i, out in enumerate(outs):
        acc = None
        for fac, rows in ((mine, kept), (other, given)):
            lhs = jnp.concatenate([fac[s, first + i] for s in range(fac.shape[0])], axis=0)
            term = lax.dot_general(lhs, rows[...], down, preferred_element_type=jnp.float32)
            acc = term if acc is None else acc + term
        out[...] = acc.astype(out.dtype)


def factors(pre_gate, pre_up, tan_gate, tan_up, back):
    sig = jax.nn.sigmoid(pre_gate)
    slope = sig * (1.0 + pre_gate * (1.0 - sig))
    bend = sig * (1.0 - sig) * (2.0 + pre_gate * (1.0 - 2.0 * sig))
    fac_gate = (back * (tan_up * slope + pre_up * bend * tan_gate)).astype(jnp.bfloat16)
    fac_up = (back * slope * tan_gate).astype(jnp.bfloat16)
    return (fac_gate, fac_up)


def stacked(parts, rows):
    row, out = 0, None
    for part in parts:
        padded = lax.pad(
            part, jnp.zeros((), part.dtype),
            ((row, rows - row - part.shape[0], 0), (0, 0, 0)),
        )
        out = padded if out is None else out + padded
        row += part.shape[0]
    return out


def on_device(
    tokens, cotangent, gate_weight, up_weight, down_weight, gate_probe, up_probe, interpret
):
    nx, ny, nzl = lax.axis_size("x"), lax.axis_size("y"), lax.axis_size("zl")
    own, feats = tokens.shape
    hid = gate_weight.shape[0]
    total = own * lax.axis_size(("zh", "x", "y"))
    zl, core = lax.axis_index("zl"), lax.axis_index("c")

    rows = stacked([tokens, cotangent], 2 * own)
    block = jnp.stack([rows, swap(rows, "zh")], axis=0)

    tok_rows, cot_rows = 4 * hid, hid * 8 // 7
    mats = stacked(
        [gate_weight, up_weight, gate_probe, up_probe, down_weight], tok_rows + cot_rows
    )
    weights = [mats] + [shift(mats, "x", by) for by in range(1, nx)]

    ahead = behind = block
    blocks = [block]
    for _ in range(ny // 2 - 1):
        ahead, behind = shift(ahead, "y", 1), shift(behind, "y", -1)
        blocks += [ahead, behind]
    blocks += [shift(ahead[:1], "y", 1), shift(behind[1:], "y", -1)]

    count = ny * own
    cut, columns = nx * tok_rows, nx * (tok_rows + cot_rows)
    term = functools.partial(
        local_call,
        functools.partial(terms_kernel, own, tok_rows),
        (
            jax.ShapeDtypeStruct((count, columns), jnp.float32),
            jax.ShapeDtypeStruct((count, feats), jnp.bfloat16),
        ),
        2 * count * columns * feats,
        2 * columns * feats,
        interpret,
        in_specs=[SMEM] + [ANY] * (len(blocks) + nx),
        out_specs=(VMEM, VMEM),
        scratch_shapes=[
            pltpu.VMEM((count, feats), jnp.bfloat16),
            pltpu.VMEM((columns, feats), jnp.bfloat16),
            pltpu.SemaphoreType.DMA((4 * ny,)),
            pltpu.SemaphoreType.DMA((2 * nx,)),
        ],
    )
    given, given_rows = term(jnp.stack([1 - core, zl]), *blocks, *weights)
    other = swap(given, "c")
    kept, kept_rows = term(jnp.stack([core, zl]), *blocks, *weights)
    terms = kept + other

    column = np.arange(columns)
    scale = np.where(
        column >= cut,
        BACK_SCALE,
        np.where(column % tok_rows >= 2 * hid, TAN_SCALE, PRE_SCALE),
    ).astype(np.float32)
    share = count // nzl
    sent = (terms[share:] * scale).astype(jnp.float16)
    got = [
        mix(sent[(by - 1) * share : by * share], "zl", by).astype(jnp.float32)
        for by in range(1, nzl)
    ]
    proj = terms[:share] + sum(got) * (1.0 / scale)
    tok_part = proj[:, :cut].reshape(share, nx, 4, hid)
    back = proj[:, cut:].reshape(share, nx, cot_rows)[:, :, :hid]
    fac = jnp.concatenate(factors(*[tok_part[:, :, i] for i in range(4)], back), axis=2)

    fac = fac.transpose(1, 0, 2)
    fac = jnp.stack([fac] + [mix(fac, "zl", by) for by in range(1, nzl)], axis=0)
    fac_other = swap(fac, "c")

    def hvp(first, kinds):
        return local_call(
            functools.partial(hvp_kernel, first),
            tuple(jax.ShapeDtypeStruct((2 * hid, feats), kind) for kind in kinds),
            8 * len(kinds) * hid * count * feats,
            4 * count * feats,
            interpret,
            fac,
            fac_other,
            kept_rows,
            given_rows,
            in_specs=[VMEM] * 4,
            out_specs=(VMEM,) * len(kinds),
        )
    away = hvp(1, [jnp.bfloat16] * (nx - 1))
    away = [shift(part, "x", -by) for by, part in enumerate(away, 1)]
    (both,) = hvp(0, [jnp.float32])
    both = (both + sum(part.astype(jnp.float32) for part in away)) / total
    gate_diag = gate_probe.astype(jnp.float32) * both[:hid]
    up_diag = up_probe.astype(jnp.float32) * both[hid:]
    return (gate_diag, up_diag)


def solution(mesh, interpret=False):
    sizes = {**NODE, **LOCAL}
    cut = Mesh(mesh.devices.reshape(tuple(sizes.values())), tuple(sizes))
    placed = P(tuple(NODE), tuple(LOCAL))
    return jax.shard_map(
        functools.partial(on_device, interpret=interpret),
        mesh=cut,
        in_specs=(placed,) * 7,
        out_specs=(placed, placed),
        check_vma=False,
    )
```

```python
import functools

import jax
import jax.numpy as jnp
from jax import lax
from jax.experimental import pallas as pl
from jax.experimental.pallas import tpu as pltpu
from jax.sharding import Mesh, PartitionSpec as P

NODE = {"zh": 2, "x": 4, "y": 8}
LOCAL = {"zl": 4, "c": 2}

PRE_SCALE = 64.0
TAN_SCALE = 0.5
BACK_SCALE = 32.0

VMEM = pl.BlockSpec(memory_space=pltpu.VMEM)
SMEM = pl.BlockSpec(memory_space=pltpu.SMEM)


def swap(value, axis):
    return lax.ppermute(value, axis, [(0, 1), (1, 0)])


def shift(value, axis, by):
    size = lax.axis_size(axis)
    return lax.ppermute(value, axis, [(i, (i + by) % size) for i in range(size)])


def mix(value, axis, by):
    return lax.ppermute(value, axis, [(i, i ^ by) for i in range(lax.axis_size(axis))])


def local_call(body, out_shape, flops, moved, interpret, *args, **options):
    return pl.pallas_call(
        body,
        out_shape=out_shape,
        cost_estimate=pl.CostEstimate(flops=flops, bytes_accessed=moved, transcendentals=0),
        compiler_params=pltpu.CompilerParams(vmem_limit_bytes=16 * 1024 * 1024),
        interpret=interpret,
        **options,
    )(*args)


def terms_kernel(tok_rows, place, tokens, cotangents, *refs):
    *weights, out, w_all = refs
    cut = len(weights) * tok_rows
    cot_rows = weights[0].shape[0] - tok_rows
    for i, weight in enumerate(weights):
        w_all[i * tok_rows : (i + 1) * tok_rows] = weight[:tok_rows]
        start = cut + i * cot_rows
        w_all[start : start + cot_rows] = weight[tok_rows:]
    count = out.shape[0]
    half = pl.ds(pl.multiple_of(place[0] * count, count), count)
    across = (((1,), (1,)), ((), ()))
    column = lax.rem(lax.broadcasted_iota(jnp.int32, (1, cut), 1), tok_rows)
    out[:, :cut] = lax.dot_general(
        tokens[half], w_all[:cut], across, preferred_element_type=jnp.float32
    ) * jnp.where(column * 2 >= tok_rows, TAN_SCALE, PRE_SCALE)
    out[:, cut:] = BACK_SCALE * lax.dot_general(
        cotangents[half], w_all[cut:], across, preferred_element_type=jnp.float32
    )


def hvp_kernel(nzl, nc, place, fac, tokens, away, own):
    nx, width, _ = away.shape
    lanes = fac.shape[1] // (nzl * nc * nx)
    for i in range(nx):
        step = place[0] ^ i
        step = step ^ (step >> 1)
        parts = []
        for c in range(nc):
            for z in range(nzl):
                start = pl.multiple_of(((z * nc + c) * nx + step) * lanes, lanes)
                parts.append(fac[:, pl.ds(start, lanes)])
        term = lax.dot_general(
            jnp.concatenate(parts, axis=0), tokens[...], (((0,), (0,)), ((), ())),
            preferred_element_type=jnp.float32,
        )[:width]
        away[i] = term.astype(away.dtype)

        @pl.when(place[0] == i)
        def _():
            own[...] = term


def sum_kernel(total, place, away, own, gate_probe, up_probe, gate_diag, up_diag):
    both = own[...]
    for i in range(away.shape[0]):
        both += jnp.where(place[0] == i, 0.0, away[i].astype(jnp.float32))
    both = both / total
    hid = gate_diag.shape[0]
    gate_diag[...] = gate_probe[...].astype(jnp.float32) * both[:hid]
    up_diag[...] = up_probe[...].astype(jnp.float32) * both[hid:]


def factors(pre_gate, pre_up, tan_gate, tan_up, back):
    sig = jax.nn.sigmoid(pre_gate)
    slope = sig * (1.0 + pre_gate * (1.0 - sig))
    bend = sig * (1.0 - sig) * (2.0 + pre_gate * (1.0 - 2.0 * sig))
    fac_gate = (back * (tan_up * slope + pre_up * bend * tan_gate)).astype(jnp.bfloat16)
    fac_up = (back * slope * tan_gate).astype(jnp.bfloat16)
    return (fac_gate, fac_up)


def stacked(parts, rows):
    row, out = 0, None
    for part in parts:
        padded = lax.pad(
            part, jnp.zeros((), part.dtype),
            ((row, rows - row - part.shape[0], 0), (0, 0, 0)),
        )
        out = padded if out is None else out + padded
        row += part.shape[0]
    return out


def on_device(
    tokens, cotangent, gate_weight, up_weight, down_weight, gate_probe, up_probe, interpret
):
    nx, ny, nzl = lax.axis_size("x"), lax.axis_size("y"), lax.axis_size("zl")
    own, feats = tokens.shape
    hid = gate_weight.shape[0]
    total = own * lax.axis_size(("zh", "x", "y"))
    nc = lax.axis_size("c")
    x, core = lax.axis_index("x"), lax.axis_index("c")

    rows = stacked([tokens, cotangent], 2 * own)
    block = jnp.stack([rows, swap(rows, "zh")], axis=0)

    tok_rows, cot_rows = 4 * hid, hid * 8 // 7
    mats = stacked(
        [gate_weight, up_weight, gate_probe, up_probe, down_weight], tok_rows + cot_rows
    )
    beside = mix(mats, "x", 1)
    weights = [mats, beside, mix(mats, "x", 3), mix(beside, "x", 3)]

    ahead = behind = block
    blocks = [block]
    for _ in range(ny // 2 - 1):
        ahead, behind = shift(ahead, "y", 1), shift(behind, "y", -1)
        blocks += [ahead, behind]
    blocks += [shift(ahead[:1], "y", 1), shift(behind[1:], "y", -1)]
    tok_all = jnp.concatenate([b[:, :own] for b in blocks], axis=0).reshape(-1, feats)
    cot_all = jnp.concatenate([b[:, own:] for b in blocks], axis=0).reshape(-1, feats)

    count = tok_all.shape[0] // nc
    cut, columns = nx * tok_rows, nx * (tok_rows + cot_rows)
    def term(which):
        return local_call(
            functools.partial(terms_kernel, tok_rows),
            jax.ShapeDtypeStruct((count, columns), jnp.float32),
            2 * count * columns * feats,
            2 * columns * feats,
            interpret,
            which.reshape(1),
            tok_all,
            cot_all,
            *weights,
            in_specs=[SMEM] + [VMEM] * (2 + nx),
            out_specs=VMEM,
            scratch_shapes=[pltpu.VMEM((columns, feats), jnp.bfloat16)],
        )
    other = swap(term(1 - core), "c")
    terms = term(core) + other

    share = count // nzl
    sent = terms.astype(jnp.float16).reshape(nzl, share, columns)
    got = lax.all_to_all(sent, "zl", 0, 0, tiled=True)
    proj = jnp.sum(got.astype(jnp.float32), axis=0)
    tok_part = proj[:, :cut].reshape(share, nx, 4, hid)
    pre_gate, pre_up = (tok_part[:, :, i] * (1.0 / PRE_SCALE) for i in (0, 1))
    tan_gate, tan_up = (tok_part[:, :, i] * (1.0 / TAN_SCALE) for i in (2, 3))
    back = proj[:, cut:].reshape(share, nx, cot_rows)[:, :, :hid] * (1.0 / BACK_SCALE)
    fac_gate, fac_up = factors(pre_gate, pre_up, tan_gate, tan_up, back)

    lanes = -(-2 * hid // 128) * 128
    fill = fac_up[:, :, : lanes - 2 * hid]
    fac = jnp.concatenate([fac_gate, fac_up, fill], axis=2).reshape(share, nx * lanes)
    fac = lax.all_gather(fac, ("zl", "c"), axis=1, tiled=True)

    away, mine = local_call(
        functools.partial(hvp_kernel, nzl, nc),
        (
            jax.ShapeDtypeStruct((nx, 2 * hid, feats), jnp.bfloat16),
            jax.ShapeDtypeStruct((2 * hid, feats), jnp.float32),
        ),
        4 * nx * hid * nc * count * feats,
        2 * nc * count * feats,
        interpret,
        x.reshape(1),
        fac,
        tok_all,
        in_specs=[SMEM, VMEM, VMEM],
        out_specs=(VMEM, VMEM),
    )
    away = lax.all_to_all(away, "x", 0, 0, tiled=True)
    diag = jax.ShapeDtypeStruct((hid, feats), jnp.float32)
    return local_call(
        functools.partial(sum_kernel, total),
        (diag, diag),
        2 * nx * hid * feats,
        8 * nx * hid * feats,
        interpret,
        x.reshape(1),
        away,
        mine,
        gate_probe,
        up_probe,
        in_specs=[SMEM] + [VMEM] * 4,
        out_specs=(VMEM, VMEM),
    )


def solution(mesh, interpret=False):
    sizes = {**NODE, **LOCAL}
    cut = Mesh(mesh.devices.reshape(tuple(sizes.values())), tuple(sizes))
    placed = P(tuple(NODE), tuple(LOCAL))
    return jax.shard_map(
        functools.partial(on_device, interpret=interpret),
        mesh=cut,
        in_specs=(placed,) * 7,
        out_specs=(placed, placed),
        check_vma=False,
    )
```

```python
import functools

import jax
import jax.numpy as jnp
from jax import lax
from jax.experimental import pallas as pl
from jax.experimental.pallas import tpu as pltpu
from jax.sharding import Mesh, PartitionSpec as P

NODE = {"zh": 2, "x": 4, "y": 8}
LOCAL = {"zl": 4, "c": 2}

PRE_SCALE = 64.0
TAN_SCALE = 0.5
BACK_SCALE = 32.0

VMEM = pl.BlockSpec(memory_space=pltpu.VMEM)
SMEM = pl.BlockSpec(memory_space=pltpu.SMEM)


def swap(value, axis):
    return lax.ppermute(value, axis, [(0, 1), (1, 0)])


def shift(value, axis, by):
    size = lax.axis_size(axis)
    return lax.ppermute(value, axis, [(i, (i + by) % size) for i in range(size)])


def mix(value, axis, by):
    return lax.ppermute(value, axis, [(i, i ^ by) for i in range(lax.axis_size(axis))])


def local_call(body, out_shape, flops, moved, interpret, *args, **options):
    return pl.pallas_call(
        body,
        out_shape=out_shape,
        cost_estimate=pl.CostEstimate(flops=flops, bytes_accessed=moved, transcendentals=0),
        compiler_params=pltpu.CompilerParams(vmem_limit_bytes=16 * 1024 * 1024),
        interpret=interpret,
        **options,
    )(*args)


def terms_kernel(tok_rows, which, place, tokens, cotangents, *refs):
    *weights, out, w_all = refs
    cut = len(weights) * tok_rows
    cot_rows = weights[0].shape[0] - tok_rows
    for i, weight in enumerate(weights):
        w_all[i * tok_rows : (i + 1) * tok_rows] = weight[:tok_rows]
        start = cut + i * cot_rows
        w_all[start : start + cot_rows] = weight[tok_rows:]
    count = out.shape[0]
    half = pl.ds(pl.multiple_of(place[which] * count, count), count)
    across = (((1,), (1,)), ((), ()))
    column = lax.rem(lax.broadcasted_iota(jnp.int32, (1, cut), 1), tok_rows)
    out[:, :cut] = lax.dot_general(
        tokens[half], w_all[:cut], across, preferred_element_type=jnp.float32
    ) * jnp.where(column * 2 >= tok_rows, TAN_SCALE, PRE_SCALE)
    out[:, cut:] = BACK_SCALE * lax.dot_general(
        cotangents[half], w_all[cut:], across, preferred_element_type=jnp.float32
    )


def hvp_kernel(nzl, nc, place, fac, tokens, away, own):
    nx, width, _ = away.shape
    lanes = fac.shape[1] // (nzl * nc * nx)
    for i in range(nx):
        step = place[2] ^ i
        step = step ^ (step >> 1)
        parts = []
        for c in range(nc):
            for z in range(nzl):
                start = pl.multiple_of(((z * nc + c) * nx + step) * lanes, lanes)
                parts.append(fac[:, pl.ds(start, lanes)])
        term = lax.dot_general(
            jnp.concatenate(parts, axis=0), tokens[...], (((0,), (0,)), ((), ())),
            preferred_element_type=jnp.float32,
        )[:width]
        away[i] = term.astype(away.dtype)

        @pl.when(place[2] == i)
        def _():
            own[...] = term


def sum_kernel(total, place, away, own, gate_probe, up_probe, gate_diag, up_diag):
    both = own[...]
    for i in range(away.shape[0]):
        both += jnp.where(place[2] == i, 0.0, away[i].astype(jnp.float32))
    both = both / total
    hid = gate_diag.shape[0]
    gate_diag[...] = gate_probe[...].astype(jnp.float32) * both[:hid]
    up_diag[...] = up_probe[...].astype(jnp.float32) * both[hid:]


def factors(pre_gate, pre_up, tan_gate, tan_up, back):
    sig = jax.nn.sigmoid(pre_gate)
    slope = sig * (1.0 + pre_gate * (1.0 - sig))
    bend = sig * (1.0 - sig) * (2.0 + pre_gate * (1.0 - 2.0 * sig))
    fac_gate = (back * (tan_up * slope + pre_up * bend * tan_gate)).astype(jnp.bfloat16)
    fac_up = (back * slope * tan_gate).astype(jnp.bfloat16)
    return (fac_gate, fac_up)


def stacked(parts, rows):
    row, out = 0, None
    for part in parts:
        padded = lax.pad(
            part, jnp.zeros((), part.dtype),
            ((row, rows - row - part.shape[0], 0), (0, 0, 0)),
        )
        out = padded if out is None else out + padded
        row += part.shape[0]
    return out


def on_device(
    tokens, cotangent, gate_weight, up_weight, down_weight, gate_probe, up_probe, interpret
):
    nx, ny, nzl = lax.axis_size("x"), lax.axis_size("y"), lax.axis_size("zl")
    own, feats = tokens.shape
    hid = gate_weight.shape[0]
    total = own * lax.axis_size(("zh", "x", "y"))
    nc = lax.axis_size("c")
    core = lax.axis_index("c")
    place = jnp.stack([core, 1 - core, lax.axis_index("x")])

    rows = stacked([tokens, cotangent], 2 * own)
    block = jnp.stack([rows, swap(rows, "zh")], axis=0)

    tok_rows, cot_rows = 4 * hid, hid * 8 // 7
    mats = stacked(
        [gate_weight, up_weight, gate_probe, up_probe, down_weight], tok_rows + cot_rows
    )
    beside = mix(mats, "x", 1)
    weights = [mats, beside, mix(mats, "x", 3), mix(beside, "x", 3)]

    ahead = behind = block
    blocks = [block]
    for _ in range(ny // 2 - 1):
        ahead, behind = shift(ahead, "y", 1), shift(behind, "y", -1)
        blocks += [ahead, behind]
    blocks += [shift(ahead[:1], "y", 1), shift(behind[1:], "y", -1)]
    tok_all = jnp.concatenate([b[:, :own] for b in blocks], axis=0).reshape(-1, feats)
    cot_all = jnp.concatenate([b[:, own:] for b in blocks], axis=0).reshape(-1, feats)

    count = tok_all.shape[0] // nc
    cut, columns = nx * tok_rows, nx * (tok_rows + cot_rows)
    def term(which):
        return local_call(
            functools.partial(terms_kernel, tok_rows, which),
            jax.ShapeDtypeStruct((count, columns), jnp.float32),
            2 * count * columns * feats,
            2 * columns * feats,
            interpret,
            place,
            tok_all,
            cot_all,
            *weights,
            in_specs=[SMEM] + [VMEM] * (2 + nx),
            out_specs=VMEM,
            scratch_shapes=[pltpu.VMEM((columns, feats), jnp.bfloat16)],
        )
    other = swap(term(1), "c")
    terms = term(0) + other

    share = count // nzl
    sent = terms.astype(jnp.float16).reshape(nzl, share, columns)
    got = lax.all_to_all(sent, "zl", 0, 0, tiled=True)
    proj = jnp.sum(got.astype(jnp.float32), axis=0)
    tok_part = proj[:, :cut].reshape(share, nx, 4, hid)
    pre_gate, pre_up = (tok_part[:, :, i] * (1.0 / PRE_SCALE) for i in (0, 1))
    tan_gate, tan_up = (tok_part[:, :, i] * (1.0 / TAN_SCALE) for i in (2, 3))
    back = proj[:, cut:].reshape(share, nx, cot_rows)[:, :, :hid] * (1.0 / BACK_SCALE)
    fac_gate, fac_up = factors(pre_gate, pre_up, tan_gate, tan_up, back)

    lanes = -(-2 * hid // 128) * 128
    fill = fac_up[:, :, : lanes - 2 * hid]
    fac = jnp.concatenate([fac_gate, fac_up, fill], axis=2).reshape(share, nx * lanes)
    fac = lax.all_gather(fac, ("zl", "c"), axis=1, tiled=True)

    away, mine = local_call(
        functools.partial(hvp_kernel, nzl, nc),
        (
            jax.ShapeDtypeStruct((nx, 2 * hid, feats), jnp.bfloat16),
            jax.ShapeDtypeStruct((2 * hid, feats), jnp.float32),
        ),
        4 * nx * hid * nc * count * feats,
        2 * nc * count * feats,
        interpret,
        place,
        fac,
        tok_all,
        in_specs=[SMEM, VMEM, VMEM],
        out_specs=(VMEM, VMEM),
    )
    away = lax.all_to_all(away, "x", 0, 0, tiled=True)
    diag = jax.ShapeDtypeStruct((hid, feats), jnp.float32)
    return local_call(
        functools.partial(sum_kernel, total),
        (diag, diag),
        2 * nx * hid * feats,
        8 * nx * hid * feats,
        interpret,
        place,
        away,
        mine,
        gate_probe,
        up_probe,
        in_specs=[SMEM] + [VMEM] * 4,
        out_specs=(VMEM, VMEM),
    )


def solution(mesh, interpret=False):
    sizes = {**NODE, **LOCAL}
    cut = Mesh(mesh.devices.reshape(tuple(sizes.values())), tuple(sizes))
    placed = P(tuple(NODE), tuple(LOCAL))
    return jax.shard_map(
        functools.partial(on_device, interpret=interpret),
        mesh=cut,
        in_specs=(placed,) * 7,
        out_specs=(placed, placed),
        check_vma=False,
    )
```

```python
import functools

import jax
import jax.numpy as jnp
from jax import lax
from jax.experimental import pallas as pl
from jax.experimental.pallas import tpu as pltpu
from jax.sharding import Mesh, PartitionSpec as P

NODE = {"zh": 2, "x": 4, "y": 8}
LOCAL = {"zl": 4, "c": 2}

PRE_SCALE = 64.0
TAN_SCALE = 0.5
BACK_SCALE = 32.0

VMEM = pl.BlockSpec(memory_space=pltpu.VMEM)
ANY = pl.BlockSpec(memory_space=pl.ANY)
SMEM = pl.BlockSpec(memory_space=pltpu.SMEM)


def swap(value, axis):
    return lax.ppermute(value, axis, [(0, 1), (1, 0)])


def shift(value, axis, by):
    size = lax.axis_size(axis)
    return lax.ppermute(value, axis, [(i, (i + by) % size) for i in range(size)])


def mix(value, axis, by):
    return lax.ppermute(value, axis, [(i, i ^ by) for i in range(lax.axis_size(axis))])


def local_call(body, out_shape, flops, moved, interpret, *args, **options):
    return pl.pallas_call(
        body,
        out_shape=out_shape,
        cost_estimate=pl.CostEstimate(flops=flops, bytes_accessed=moved, transcendentals=0),
        compiler_params=pltpu.CompilerParams(vmem_limit_bytes=16 * 1024 * 1024),
        interpret=interpret,
        **options,
    )(*args)


def pass_kernel(value, *rest):
    pass


def after(value, others, interpret):
    return local_call(
        pass_kernel,
        jax.ShapeDtypeStruct(value.shape, value.dtype),
        0,
        0,
        interpret,
        value,
        *others,
        in_specs=[ANY] * (1 + len(others)),
        out_specs=ANY,
        input_output_aliases={0: 0},
    )


def terms_kernel(tok_rows, place, tokens, cotangents, *refs):
    *weights, out, w_all = refs
    cut = len(weights) * tok_rows
    cot_rows = weights[0].shape[0] - tok_rows
    for i, weight in enumerate(weights):
        w_all[i * tok_rows : (i + 1) * tok_rows] = weight[:tok_rows]
        start = cut + i * cot_rows
        w_all[start : start + cot_rows] = weight[tok_rows:]
    count = out.shape[0]
    half = pl.ds(pl.multiple_of(place[0] * count, count), count)
    across = (((1,), (1,)), ((), ()))
    column = lax.rem(lax.broadcasted_iota(jnp.int32, (1, cut), 1), tok_rows)
    out[:, :cut] = lax.dot_general(
        tokens[half], w_all[:cut], across, preferred_element_type=jnp.float32
    ) * jnp.where(column * 2 >= tok_rows, TAN_SCALE, PRE_SCALE)
    out[:, cut:] = BACK_SCALE * lax.dot_general(
        cotangents[half], w_all[cut:], across, preferred_element_type=jnp.float32
    )


def hvp_kernel(nzl, nc, place, fac, tokens, away, own):
    nx, width, _ = away.shape
    lanes = fac.shape[1] // (nzl * nc * nx)
    for i in range(nx):
        step = place[0] ^ i
        step = step ^ (step >> 1)
        parts = []
        for c in range(nc):
            for z in range(nzl):
                start = pl.multiple_of(((z * nc + c) * nx + step) * lanes, lanes)
                parts.append(fac[:, pl.ds(start, lanes)])
        term = lax.dot_general(
            jnp.concatenate(parts, axis=0), tokens[...], (((0,), (0,)), ((), ())),
            preferred_element_type=jnp.float32,
        )[:width]
        away[i] = term.astype(away.dtype)

        @pl.when(place[0] == i)
        def _():
            own[...] = term


def sum_kernel(total, place, away, own, gate_probe, up_probe, gate_diag, up_diag):
    both = own[...]
    for i in range(away.shape[0]):
        both += jnp.where(place[0] == i, 0.0, away[i].astype(jnp.float32))
    both = both / total
    hid = gate_diag.shape[0]
    gate_diag[...] = gate_probe[...].astype(jnp.float32) * both[:hid]
    up_diag[...] = up_probe[...].astype(jnp.float32) * both[hid:]


def factors(pre_gate, pre_up, tan_gate, tan_up, back):
    sig = jax.nn.sigmoid(pre_gate)
    slope = sig * (1.0 + pre_gate * (1.0 - sig))
    bend = sig * (1.0 - sig) * (2.0 + pre_gate * (1.0 - 2.0 * sig))
    fac_gate = (back * (tan_up * slope + pre_up * bend * tan_gate)).astype(jnp.bfloat16)
    fac_up = (back * slope * tan_gate).astype(jnp.bfloat16)
    return (fac_gate, fac_up)


def stacked(parts, rows):
    row, out = 0, None
    for part in parts:
        padded = lax.pad(
            part, jnp.zeros((), part.dtype),
            ((row, rows - row - part.shape[0], 0), (0, 0, 0)),
        )
        out = padded if out is None else out + padded
        row += part.shape[0]
    return out


def on_device(
    tokens, cotangent, gate_weight, up_weight, down_weight, gate_probe, up_probe, interpret
):
    nx, ny, nzl = lax.axis_size("x"), lax.axis_size("y"), lax.axis_size("zl")
    own, feats = tokens.shape
    hid = gate_weight.shape[0]
    total = own * lax.axis_size(("zh", "x", "y"))
    nc = lax.axis_size("c")
    x, core = lax.axis_index("x"), lax.axis_index("c")

    rows = stacked([tokens, cotangent], 2 * own)
    block = jnp.stack([rows, swap(rows, "zh")], axis=0)

    tok_rows, cot_rows = 4 * hid, hid * 8 // 7
    mats = stacked(
        [gate_weight, up_weight, gate_probe, up_probe, down_weight], tok_rows + cot_rows
    )
    beside = mix(mats, "x", 1)
    weights = [mats, beside, mix(mats, "x", 3), mix(beside, "x", 3)]

    ahead = behind = block
    blocks = [block]
    for step in range(ny // 2 - 1):
        if step == 1:
            ahead = after(ahead, weights[1:3], interpret)
        ahead, behind = shift(ahead, "y", 1), shift(behind, "y", -1)
        blocks += [ahead, behind]
    blocks += [shift(ahead[:1], "y", 1), shift(behind[1:], "y", -1)]
    tok_all = jnp.concatenate([b[:, :own] for b in blocks], axis=0).reshape(-1, feats)
    cot_all = jnp.concatenate([b[:, own:] for b in blocks], axis=0).reshape(-1, feats)

    count = tok_all.shape[0] // nc
    cut, columns = nx * tok_rows, nx * (tok_rows + cot_rows)
    def term(which):
        return local_call(
            functools.partial(terms_kernel, tok_rows),
            jax.ShapeDtypeStruct((count, columns), jnp.float32),
            2 * count * columns * feats,
            2 * columns * feats,
            interpret,
            which.reshape(1),
            tok_all,
            cot_all,
            *weights,
            in_specs=[SMEM] + [VMEM] * (2 + nx),
            out_specs=VMEM,
            scratch_shapes=[pltpu.VMEM((columns, feats), jnp.bfloat16)],
        )
    other = swap(term(1 - core), "c")
    terms = term(core) + other

    share = count // nzl
    sent = terms.astype(jnp.float16).reshape(nzl, share, columns)
    got = lax.all_to_all(sent, "zl", 0, 0, tiled=True)
    proj = jnp.sum(got.astype(jnp.float32), axis=0)
    tok_part = proj[:, :cut].reshape(share, nx, 4, hid)
    pre_gate, pre_up = (tok_part[:, :, i] * (1.0 / PRE_SCALE) for i in (0, 1))
    tan_gate, tan_up = (tok_part[:, :, i] * (1.0 / TAN_SCALE) for i in (2, 3))
    back = proj[:, cut:].reshape(share, nx, cot_rows)[:, :, :hid] * (1.0 / BACK_SCALE)
    fac_gate, fac_up = factors(pre_gate, pre_up, tan_gate, tan_up, back)

    lanes = -(-2 * hid // 128) * 128
    fill = fac_up[:, :, : lanes - 2 * hid]
    fac = jnp.concatenate([fac_gate, fac_up, fill], axis=2).reshape(share, nx * lanes)
    fac = lax.all_gather(fac, ("zl", "c"), axis=1, tiled=True)

    away, mine = local_call(
        functools.partial(hvp_kernel, nzl, nc),
        (
            jax.ShapeDtypeStruct((nx, 2 * hid, feats), jnp.bfloat16),
            jax.ShapeDtypeStruct((2 * hid, feats), jnp.float32),
        ),
        4 * nx * hid * nc * count * feats,
        2 * nc * count * feats,
        interpret,
        x.reshape(1),
        fac,
        tok_all,
        in_specs=[SMEM, VMEM, VMEM],
        out_specs=(VMEM, VMEM),
    )
    away = lax.all_to_all(away, "x", 0, 0, tiled=True)
    diag = jax.ShapeDtypeStruct((hid, feats), jnp.float32)
    return local_call(
        functools.partial(sum_kernel, total),
        (diag, diag),
        2 * nx * hid * feats,
        8 * nx * hid * feats,
        interpret,
        x.reshape(1),
        away,
        mine,
        gate_probe,
        up_probe,
        in_specs=[SMEM] + [VMEM] * 4,
        out_specs=(VMEM, VMEM),
    )


def solution(mesh, interpret=False):
    sizes = {**NODE, **LOCAL}
    cut = Mesh(mesh.devices.reshape(tuple(sizes.values())), tuple(sizes))
    placed = P(tuple(NODE), tuple(LOCAL))
    return jax.shard_map(
        functools.partial(on_device, interpret=interpret),
        mesh=cut,
        in_specs=(placed,) * 7,
        out_specs=(placed, placed),
        check_vma=False,
    )
```

```python
import functools

import jax
import jax.numpy as jnp
from jax import lax
from jax.experimental import pallas as pl
from jax.experimental.pallas import tpu as pltpu
from jax.sharding import Mesh, PartitionSpec as P

NODE = {"zh": 2, "x": 4, "y": 8}
LOCAL = {"zl": 4, "c": 2}

PRE_SCALE = 64.0
TAN_SCALE = 0.5
BACK_SCALE = 32.0

VMEM = pl.BlockSpec(memory_space=pltpu.VMEM)
ANY = pl.BlockSpec(memory_space=pl.ANY)
SMEM = pl.BlockSpec(memory_space=pltpu.SMEM)


def swap(value, axis):
    return lax.ppermute(value, axis, [(0, 1), (1, 0)])


def shift(value, axis, by):
    size = lax.axis_size(axis)
    return lax.ppermute(value, axis, [(i, (i + by) % size) for i in range(size)])


def mix(value, axis, by):
    return lax.ppermute(value, axis, [(i, i ^ by) for i in range(lax.axis_size(axis))])


def local_call(body, out_shape, flops, moved, interpret, *args, **options):
    return pl.pallas_call(
        body,
        out_shape=out_shape,
        cost_estimate=pl.CostEstimate(flops=flops, bytes_accessed=moved, transcendentals=0),
        compiler_params=pltpu.CompilerParams(vmem_limit_bytes=16 * 1024 * 1024),
        interpret=interpret,
        **options,
    )(*args)


def pass_kernel(value, *rest):
    pass


def after(value, others, interpret):
    return local_call(
        pass_kernel,
        jax.ShapeDtypeStruct(value.shape, value.dtype),
        0,
        0,
        interpret,
        value,
        *others,
        in_specs=[ANY] * (1 + len(others)),
        out_specs=ANY,
        input_output_aliases={0: 0},
    )


def terms_kernel(tok_rows, place, tokens, cotangents, *refs):
    *weights, out, w_all = refs
    cut = len(weights) * tok_rows
    cot_rows = weights[0].shape[0] - tok_rows
    for i, weight in enumerate(weights):
        w_all[i * tok_rows : (i + 1) * tok_rows] = weight[:tok_rows]
        start = cut + i * cot_rows
        w_all[start : start + cot_rows] = weight[tok_rows:]
    count = out.shape[0]
    half = pl.ds(pl.multiple_of(place[0] * count, count), count)
    across = (((1,), (1,)), ((), ()))
    column = lax.rem(lax.broadcasted_iota(jnp.int32, (1, cut), 1), tok_rows)
    out[:, :cut] = lax.dot_general(
        tokens[half], w_all[:cut], across, preferred_element_type=jnp.float32
    ) * jnp.where(column * 2 >= tok_rows, TAN_SCALE, PRE_SCALE)
    out[:, cut:] = BACK_SCALE * lax.dot_general(
        cotangents[half], w_all[cut:], across, preferred_element_type=jnp.float32
    )


def hvp_kernel(nzl, nc, place, fac, tokens, away, own):
    nx, width, _ = away.shape
    lanes = fac.shape[1] // (nzl * nc * nx)
    for i in range(nx):
        step = place[0] ^ i
        step = step ^ (step >> 1)
        parts = []
        for c in range(nc):
            for z in range(nzl):
                start = pl.multiple_of(((z * nc + c) * nx + step) * lanes, lanes)
                parts.append(fac[:, pl.ds(start, lanes)])
        term = lax.dot_general(
            jnp.concatenate(parts, axis=0), tokens[...], (((0,), (0,)), ((), ())),
            preferred_element_type=jnp.float32,
        )[:width]
        away[i] = term.astype(away.dtype)

        @pl.when(place[0] == i)
        def _():
            own[...] = term


def sum_kernel(total, place, away, own, gate_probe, up_probe, gate_diag, up_diag):
    both = own[...]
    for i in range(away.shape[0]):
        both += jnp.where(place[0] == i, 0.0, away[i].astype(jnp.float32))
    both = both / total
    hid = gate_diag.shape[0]
    gate_diag[...] = gate_probe[...].astype(jnp.float32) * both[:hid]
    up_diag[...] = up_probe[...].astype(jnp.float32) * both[hid:]


def factors(pre_gate, pre_up, tan_gate, tan_up, back):
    sig = jax.nn.sigmoid(pre_gate)
    slope = sig * (1.0 + pre_gate * (1.0 - sig))
    bend = sig * (1.0 - sig) * (2.0 + pre_gate * (1.0 - 2.0 * sig))
    fac_gate = (back * (tan_up * slope + pre_up * bend * tan_gate)).astype(jnp.bfloat16)
    fac_up = (back * slope * tan_gate).astype(jnp.bfloat16)
    return (fac_gate, fac_up)


def stacked(parts, rows):
    row, out = 0, None
    for part in parts:
        padded = lax.pad(
            part, jnp.zeros((), part.dtype),
            ((row, rows - row - part.shape[0], 0), (0, 0, 0)),
        )
        out = padded if out is None else out + padded
        row += part.shape[0]
    return out


def on_device(
    tokens, cotangent, gate_weight, up_weight, down_weight, gate_probe, up_probe, interpret
):
    nx, ny, nzl = lax.axis_size("x"), lax.axis_size("y"), lax.axis_size("zl")
    own, feats = tokens.shape
    hid = gate_weight.shape[0]
    total = own * lax.axis_size(("zh", "x", "y"))
    nc = lax.axis_size("c")
    x, core = lax.axis_index("x"), lax.axis_index("c")

    rows = stacked([tokens, cotangent], 2 * own)
    block = jnp.stack([rows, swap(rows, "zh")], axis=0)

    tok_rows, cot_rows = 4 * hid, hid * 8 // 7
    mats = stacked(
        [gate_weight, up_weight, gate_probe, up_probe, down_weight], tok_rows + cot_rows
    )
    beside = mix(mats, "x", 1)
    weights = [mats, beside, mix(mats, "x", 3), mix(beside, "x", 3)]

    ahead = behind = block
    blocks = [block]
    for step in range(ny // 2 - 1):
        if step == 1:
            ahead = after(ahead, weights[2:3], interpret)
        ahead, behind = shift(ahead, "y", 1), shift(behind, "y", -1)
        blocks += [ahead, behind]
    blocks += [shift(ahead[:1], "y", 1), shift(behind[1:], "y", -1)]
    tok_all = jnp.concatenate([b[:, :own] for b in blocks], axis=0).reshape(-1, feats)
    cot_all = jnp.concatenate([b[:, own:] for b in blocks], axis=0).reshape(-1, feats)

    count = tok_all.shape[0] // nc
    cut, columns = nx * tok_rows, nx * (tok_rows + cot_rows)
    def term(which):
        return local_call(
            functools.partial(terms_kernel, tok_rows),
            jax.ShapeDtypeStruct((count, columns), jnp.float32),
            2 * count * columns * feats,
            2 * columns * feats,
            interpret,
            which.reshape(1),
            tok_all,
            cot_all,
            *weights,
            in_specs=[SMEM] + [VMEM] * (2 + nx),
            out_specs=VMEM,
            scratch_shapes=[pltpu.VMEM((columns, feats), jnp.bfloat16)],
        )
    other = swap(term(1 - core), "c")
    terms = term(core) + other

    share = count // nzl
    sent = terms.astype(jnp.float16).reshape(nzl, share, columns)
    got = lax.all_to_all(sent, "zl", 0, 0, tiled=True)
    proj = jnp.sum(got.astype(jnp.float32), axis=0)
    tok_part = proj[:, :cut].reshape(share, nx, 4, hid)
    pre_gate, pre_up = (tok_part[:, :, i] * (1.0 / PRE_SCALE) for i in (0, 1))
    tan_gate, tan_up = (tok_part[:, :, i] * (1.0 / TAN_SCALE) for i in (2, 3))
    back = proj[:, cut:].reshape(share, nx, cot_rows)[:, :, :hid] * (1.0 / BACK_SCALE)
    fac_gate, fac_up = factors(pre_gate, pre_up, tan_gate, tan_up, back)

    lanes = -(-2 * hid // 128) * 128
    fill = fac_up[:, :, : lanes - 2 * hid]
    fac = jnp.concatenate([fac_gate, fac_up, fill], axis=2).reshape(share, nx * lanes)
    fac = lax.all_gather(fac, ("zl", "c"), axis=1, tiled=True)

    away, mine = local_call(
        functools.partial(hvp_kernel, nzl, nc),
        (
            jax.ShapeDtypeStruct((nx, 2 * hid, feats), jnp.bfloat16),
            jax.ShapeDtypeStruct((2 * hid, feats), jnp.float32),
        ),
        4 * nx * hid * nc * count * feats,
        2 * nc * count * feats,
        interpret,
        x.reshape(1),
        fac,
        tok_all,
        in_specs=[SMEM, VMEM, VMEM],
        out_specs=(VMEM, VMEM),
    )
    away = lax.all_to_all(away, "x", 0, 0, tiled=True)
    diag = jax.ShapeDtypeStruct((hid, feats), jnp.float32)
    return local_call(
        functools.partial(sum_kernel, total),
        (diag, diag),
        2 * nx * hid * feats,
        8 * nx * hid * feats,
        interpret,
        x.reshape(1),
        away,
        mine,
        gate_probe,
        up_probe,
        in_specs=[SMEM] + [VMEM] * 4,
        out_specs=(VMEM, VMEM),
    )


def solution(mesh, interpret=False):
    sizes = {**NODE, **LOCAL}
    cut = Mesh(mesh.devices.reshape(tuple(sizes.values())), tuple(sizes))
    placed = P(tuple(NODE), tuple(LOCAL))
    return jax.shard_map(
        functools.partial(on_device, interpret=interpret),
        mesh=cut,
        in_specs=(placed,) * 7,
        out_specs=(placed, placed),
        check_vma=False,
    )
```

```python
import functools

import jax
import jax.numpy as jnp
from jax import lax
from jax.experimental import pallas as pl
from jax.experimental.pallas import tpu as pltpu
from jax.sharding import Mesh, PartitionSpec as P

NODE = {"zh": 2, "x": 4, "y": 8}
LOCAL = {"zl": 4, "c": 2}

PRE_SCALE = 64.0
TAN_SCALE = 0.5
BACK_SCALE = 32.0

VMEM = pl.BlockSpec(memory_space=pltpu.VMEM)
ANY = pl.BlockSpec(memory_space=pl.ANY)
SMEM = pl.BlockSpec(memory_space=pltpu.SMEM)


def swap(value, axis):
    return lax.ppermute(value, axis, [(0, 1), (1, 0)])


def shift(value, axis, by):
    size = lax.axis_size(axis)
    return lax.ppermute(value, axis, [(i, (i + by) % size) for i in range(size)])


def mix(value, axis, by):
    return lax.ppermute(value, axis, [(i, i ^ by) for i in range(lax.axis_size(axis))])


def local_call(body, out_shape, flops, moved, interpret, *args, **options):
    return pl.pallas_call(
        body,
        out_shape=out_shape,
        cost_estimate=pl.CostEstimate(flops=flops, bytes_accessed=moved, transcendentals=0),
        compiler_params=pltpu.CompilerParams(vmem_limit_bytes=16 * 1024 * 1024),
        interpret=interpret,
        **options,
    )(*args)


def pass_kernel(value, *rest):
    pass


def after(value, others, interpret):
    return local_call(
        pass_kernel,
        jax.ShapeDtypeStruct(value.shape, value.dtype),
        0,
        0,
        interpret,
        value,
        *others,
        in_specs=[ANY] * (1 + len(others)),
        out_specs=ANY,
        input_output_aliases={0: 0},
    )


def terms_kernel(tok_rows, place, tokens, cotangents, *refs):
    *weights, out, w_all, sems = refs
    cut = len(weights) * tok_rows
    cot_rows = weights[0].shape[0] - tok_rows
    copies = []
    for i, weight in enumerate(weights):
        for j, (start, rows, to) in enumerate(
            ((0, tok_rows, i * tok_rows), (tok_rows, cot_rows, cut + i * cot_rows))
        ):
            copies.append(
                pltpu.make_async_copy(
                    weight.at[pl.ds(start, rows)], w_all.at[pl.ds(to, rows)], sems.at[2 * i + j]
                )
            )
    for copy in copies:
        copy.start()
    for copy in copies:
        copy.wait()
    count = out.shape[0]
    half = pl.ds(pl.multiple_of(place[0] * count, count), count)
    across = (((1,), (1,)), ((), ()))
    column = lax.rem(lax.broadcasted_iota(jnp.int32, (1, cut), 1), tok_rows)
    out[:, :cut] = lax.dot_general(
        tokens[half], w_all[:cut], across, preferred_element_type=jnp.float32
    ) * jnp.where(column * 2 >= tok_rows, TAN_SCALE, PRE_SCALE)
    out[:, cut:] = BACK_SCALE * lax.dot_general(
        cotangents[half], w_all[cut:], across, preferred_element_type=jnp.float32
    )


def hvp_kernel(nzl, nc, place, fac, tokens, away, own):
    nx, width, _ = away.shape
    lanes = fac.shape[1] // (nzl * nc * nx)
    for i in range(nx):
        step = place[0] ^ i
        step = step ^ (step >> 1)
        parts = []
        for c in range(nc):
            for z in range(nzl):
                start = pl.multiple_of(((z * nc + c) * nx + step) * lanes, lanes)
                parts.append(fac[:, pl.ds(start, lanes)])
        term = lax.dot_general(
            jnp.concatenate(parts, axis=0), tokens[...], (((0,), (0,)), ((), ())),
            preferred_element_type=jnp.float32,
        )[:width]
        away[i] = term.astype(away.dtype)

        @pl.when(place[0] == i)
        def _():
            own[...] = term


def sum_kernel(total, place, away, own, gate_probe, up_probe, gate_diag, up_diag):
    both = own[...]
    for i in range(away.shape[0]):
        both += jnp.where(place[0] == i, 0.0, away[i].astype(jnp.float32))
    both = both / total
    hid = gate_diag.shape[0]
    gate_diag[...] = gate_probe[...].astype(jnp.float32) * both[:hid]
    up_diag[...] = up_probe[...].astype(jnp.float32) * both[hid:]


def factors(pre_gate, pre_up, tan_gate, tan_up, back):
    sig = jax.nn.sigmoid(pre_gate)
    slope = sig * (1.0 + pre_gate * (1.0 - sig))
    bend = sig * (1.0 - sig) * (2.0 + pre_gate * (1.0 - 2.0 * sig))
    fac_gate = (back * (tan_up * slope + pre_up * bend * tan_gate)).astype(jnp.bfloat16)
    fac_up = (back * slope * tan_gate).astype(jnp.bfloat16)
    return (fac_gate, fac_up)


def factors_kernel(nx, hid, cut, proj, out):
    tok_rows, cot_rows = cut // nx, (proj.shape[1] - cut) // nx
    lanes = out.shape[1] // nx
    for i in range(nx):
        start = i * tok_rows
        pre_gate, pre_up, tan_gate, tan_up = (
            proj[:, start + j * hid : start + (j + 1) * hid] for j in range(4)
        )
        start = cut + i * cot_rows
        fac_gate, fac_up = factors(
            pre_gate * (1.0 / PRE_SCALE),
            pre_up * (1.0 / PRE_SCALE),
            tan_gate * (1.0 / TAN_SCALE),
            tan_up * (1.0 / TAN_SCALE),
            proj[:, start : start + hid] * (1.0 / BACK_SCALE),
        )
        rest = jnp.zeros((out.shape[0], lanes - 2 * hid), jnp.bfloat16)
        out[:, i * lanes : (i + 1) * lanes] = jnp.concatenate([fac_gate, fac_up, rest], axis=1)


def stacked(parts, rows):
    row, out = 0, None
    for part in parts:
        padded = lax.pad(
            part, jnp.zeros((), part.dtype),
            ((row, rows - row - part.shape[0], 0), (0, 0, 0)),
        )
        out = padded if out is None else out + padded
        row += part.shape[0]
    return out


def on_device(
    tokens, cotangent, gate_weight, up_weight, down_weight, gate_probe, up_probe, interpret
):
    nx, ny, nzl = lax.axis_size("x"), lax.axis_size("y"), lax.axis_size("zl")
    own, feats = tokens.shape
    hid = gate_weight.shape[0]
    total = own * lax.axis_size(("zh", "x", "y"))
    nc = lax.axis_size("c")
    x, core = lax.axis_index("x"), lax.axis_index("c")

    rows = stacked([tokens, cotangent], 2 * own)
    block = jnp.stack([rows, swap(rows, "zh")], axis=0)

    tok_rows, cot_rows = 4 * hid, hid * 8 // 7
    mats = stacked(
        [gate_weight, up_weight, gate_probe, up_probe, down_weight], tok_rows + cot_rows
    )
    beside = mix(mats, "x", 1)
    weights = [mats, beside, mix(mats, "x", 3), mix(beside, "x", 3)]

    ahead = behind = block
    blocks = [block]
    for step in range(ny // 2 - 1):
        if step == 1:
            ahead = after(ahead, weights[2:3], interpret)
        ahead, behind = shift(ahead, "y", 1), shift(behind, "y", -1)
        blocks += [ahead, behind]
    blocks += [shift(ahead[:1], "y", 1), shift(behind[1:], "y", -1)]
    tok_all = jnp.concatenate([b[:, :own] for b in blocks], axis=0).reshape(-1, feats)
    cot_all = jnp.concatenate([b[:, own:] for b in blocks], axis=0).reshape(-1, feats)

    count = tok_all.shape[0] // nc
    cut, columns = nx * tok_rows, nx * (tok_rows + cot_rows)
    def term(which):
        return local_call(
            functools.partial(terms_kernel, tok_rows),
            jax.ShapeDtypeStruct((count, columns), jnp.float32),
            2 * count * columns * feats,
            2 * columns * feats,
            interpret,
            which.reshape(1),
            tok_all,
            cot_all,
            *weights,
            in_specs=[SMEM] + [VMEM] * 2 + [ANY] * nx,
            out_specs=VMEM,
            scratch_shapes=[
                pltpu.VMEM((columns, feats), jnp.bfloat16),
                pltpu.SemaphoreType.DMA((2 * nx,)),
            ],
        )
    other = swap(term(1 - core), "c")
    terms = term(core) + other

    share = count // nzl
    sent = terms.astype(jnp.float16).reshape(nzl, share, columns)
    got = lax.all_to_all(sent, "zl", 0, 0, tiled=True)
    proj = jnp.sum(got.astype(jnp.float32), axis=0)

    lanes = -(-2 * hid // 128) * 128
    fac = local_call(
        functools.partial(factors_kernel, nx, hid, cut),
        jax.ShapeDtypeStruct((share, nx * lanes), jnp.bfloat16),
        32 * share * nx * hid,
        8 * share * columns,
        interpret,
        proj,
        in_specs=[VMEM],
        out_specs=VMEM,
    )
    fac = lax.all_gather(fac, ("zl", "c"), axis=1, tiled=True)

    away, mine = local_call(
        functools.partial(hvp_kernel, nzl, nc),
        (
            jax.ShapeDtypeStruct((nx, 2 * hid, feats), jnp.bfloat16),
            jax.ShapeDtypeStruct((2 * hid, feats), jnp.float32),
        ),
        4 * nx * hid * nc * count * feats,
        2 * nc * count * feats,
        interpret,
        x.reshape(1),
        fac,
        tok_all,
        in_specs=[SMEM, VMEM, VMEM],
        out_specs=(VMEM, VMEM),
    )
    away = lax.all_to_all(away, "x", 0, 0, tiled=True)
    diag = jax.ShapeDtypeStruct((hid, feats), jnp.float32)
    return local_call(
        functools.partial(sum_kernel, total),
        (diag, diag),
        2 * nx * hid * feats,
        8 * nx * hid * feats,
        interpret,
        x.reshape(1),
        away,
        mine,
        gate_probe,
        up_probe,
        in_specs=[SMEM] + [VMEM] * 4,
        out_specs=(VMEM, VMEM),
    )


def solution(mesh, interpret=False):
    sizes = {**NODE, **LOCAL}
    cut = Mesh(mesh.devices.reshape(tuple(sizes.values())), tuple(sizes))
    placed = P(tuple(NODE), tuple(LOCAL))
    return jax.shard_map(
        functools.partial(on_device, interpret=interpret),
        mesh=cut,
        in_specs=(placed,) * 7,
        out_specs=(placed, placed),
        check_vma=False,
    )
```

```python
import functools

import jax
import jax.numpy as jnp
from jax import lax
from jax.experimental import pallas as pl
from jax.experimental.pallas import tpu as pltpu
from jax.sharding import Mesh, PartitionSpec as P

NODE = {"zh": 2, "x": 4, "y": 8}
LOCAL = {"zl": 4, "c": 2}

PRE_SCALE = 64.0
TAN_SCALE = 0.5
BACK_SCALE = 32.0

VMEM = pl.BlockSpec(memory_space=pltpu.VMEM)
SMEM = pl.BlockSpec(memory_space=pltpu.SMEM)


def swap(value, axis):
    return lax.ppermute(value, axis, [(0, 1), (1, 0)])


def shift(value, axis, by):
    size = lax.axis_size(axis)
    return lax.ppermute(value, axis, [(i, (i + by) % size) for i in range(size)])


def mix(value, axis, by):
    return lax.ppermute(value, axis, [(i, i ^ by) for i in range(lax.axis_size(axis))])


def local_call(body, out_shape, flops, moved, interpret, *args, **options):
    return pl.pallas_call(
        body,
        out_shape=out_shape,
        cost_estimate=pl.CostEstimate(flops=flops, bytes_accessed=moved, transcendentals=0),
        compiler_params=pltpu.CompilerParams(vmem_limit_bytes=16 * 1024 * 1024),
        interpret=interpret,
        **options,
    )(*args)


def terms_kernel(tok_rows, place, tokens, cotangents, *refs):
    *weights, out, w_all = refs
    cut = len(weights) * tok_rows
    cot_rows = weights[0].shape[0] - tok_rows
    for i, weight in enumerate(weights):
        w_all[i * tok_rows : (i + 1) * tok_rows] = weight[:tok_rows]
        start = cut + i * cot_rows
        w_all[start : start + cot_rows] = weight[tok_rows:]
    count = out.shape[0]
    half = pl.ds(pl.multiple_of(place[0] * count, count), count)
    across = (((1,), (1,)), ((), ()))
    column = lax.rem(lax.broadcasted_iota(jnp.int32, (1, cut), 1), tok_rows)
    out[:, :cut] = lax.dot_general(
        tokens[half], w_all[:cut], across, preferred_element_type=jnp.float32
    ) * jnp.where(column * 2 >= tok_rows, TAN_SCALE, PRE_SCALE)
    out[:, cut:] = BACK_SCALE * lax.dot_general(
        cotangents[half], w_all[cut:], across, preferred_element_type=jnp.float32
    )


def hvp_kernel(nzl, nc, place, fac, tokens, away, own):
    nx, width, _ = away.shape
    lanes = fac.shape[1] // (nzl * nc * nx)
    for i in range(nx):
        step = place[0] ^ i
        step = step ^ (step >> 1)
        parts = []
        for c in range(nc):
            for z in range(nzl):
                start = pl.multiple_of(((z * nc + c) * nx + step) * lanes, lanes)
                parts.append(fac[:, pl.ds(start, lanes)])
        term = lax.dot_general(
            jnp.concatenate(parts, axis=0), tokens[...], (((0,), (0,)), ((), ())),
            preferred_element_type=jnp.float32,
        )[:width]
        away[i] = term.astype(away.dtype)

        @pl.when(place[0] == i)
        def _():
            own[...] = term


def sum_kernel(total, place, away, own, gate_probe, up_probe, gate_diag, up_diag):
    both = own[...]
    for i in range(away.shape[0]):
        both += jnp.where(place[0] == i, 0.0, away[i].astype(jnp.float32))
    both = both / total
    hid = gate_diag.shape[0]
    gate_diag[...] = gate_probe[...].astype(jnp.float32) * both[:hid]
    up_diag[...] = up_probe[...].astype(jnp.float32) * both[hid:]


def factors(pre_gate, pre_up, tan_gate, tan_up, back):
    sig = jax.nn.sigmoid(pre_gate)
    slope = sig * (1.0 + pre_gate * (1.0 - sig))
    bend = sig * (1.0 - sig) * (2.0 + pre_gate * (1.0 - 2.0 * sig))
    fac_gate = (back * (tan_up * slope + pre_up * bend * tan_gate)).astype(jnp.bfloat16)
    fac_up = (back * slope * tan_gate).astype(jnp.bfloat16)
    return (fac_gate, fac_up)


def factors_kernel(nx, hid, cut, proj, out):
    tok_rows, cot_rows = cut // nx, (proj.shape[1] - cut) // nx
    lanes = out.shape[1] // nx
    for i in range(nx):
        start = i * tok_rows
        pre_gate, pre_up, tan_gate, tan_up = (
            proj[:, start + j * hid : start + (j + 1) * hid] for j in range(4)
        )
        start = cut + i * cot_rows
        fac_gate, fac_up = factors(
            pre_gate * (1.0 / PRE_SCALE),
            pre_up * (1.0 / PRE_SCALE),
            tan_gate * (1.0 / TAN_SCALE),
            tan_up * (1.0 / TAN_SCALE),
            proj[:, start : start + hid] * (1.0 / BACK_SCALE),
        )
        rest = jnp.zeros((out.shape[0], lanes - 2 * hid), jnp.bfloat16)
        out[:, i * lanes : (i + 1) * lanes] = jnp.concatenate([fac_gate, fac_up, rest], axis=1)


def stacked(parts, rows):
    row, out = 0, None
    for part in parts:
        padded = lax.pad(
            part, jnp.zeros((), part.dtype),
            ((row, rows - row - part.shape[0], 0), (0, 0, 0)),
        )
        out = padded if out is None else out + padded
        row += part.shape[0]
    return out


def on_device(
    tokens, cotangent, gate_weight, up_weight, down_weight, gate_probe, up_probe, interpret
):
    nx, ny, nzl = lax.axis_size("x"), lax.axis_size("y"), lax.axis_size("zl")
    own, feats = tokens.shape
    hid = gate_weight.shape[0]
    total = own * lax.axis_size(("zh", "x", "y"))
    nc = lax.axis_size("c")
    x, core = lax.axis_index("x"), lax.axis_index("c")

    rows = stacked([tokens, cotangent], 2 * own)
    block = jnp.stack([rows, swap(rows, "zh")], axis=0)

    tok_rows, cot_rows = 4 * hid, hid * 8 // 7
    mats = stacked(
        [gate_weight, up_weight, gate_probe, up_probe, down_weight], tok_rows + cot_rows
    )
    beside = mix(mats, "x", 1)
    weights = [mats, beside, mix(mats, "x", 3), mix(beside, "x", 3)]

    ahead = behind = block
    blocks = [block]
    for _ in range(ny // 2 - 1):
        ahead, behind = shift(ahead, "y", 1), shift(behind, "y", -1)
        blocks += [ahead, behind]
    blocks += [shift(ahead[:1], "y", 1), shift(behind[1:], "y", -1)]
    tok_all = jnp.concatenate([b[:, :own] for b in blocks], axis=0).reshape(-1, feats)
    cot_all = jnp.concatenate([b[:, own:] for b in blocks], axis=0).reshape(-1, feats)

    count = tok_all.shape[0] // nc
    cut, columns = nx * tok_rows, nx * (tok_rows + cot_rows)
    def term(which):
        return local_call(
            functools.partial(terms_kernel, tok_rows),
            jax.ShapeDtypeStruct((count, columns), jnp.float32),
            2 * count * columns * feats,
            2 * columns * feats,
            interpret,
            which.reshape(1),
            tok_all,
            cot_all,
            *weights,
            in_specs=[SMEM] + [VMEM] * (2 + nx),
            out_specs=VMEM,
            scratch_shapes=[pltpu.VMEM((columns, feats), jnp.bfloat16)],
        )
    other = swap(term(1 - core), "c")
    terms = term(core) + other

    share = count // nzl
    sent = terms.astype(jnp.float16).reshape(nzl, share, columns)
    got = lax.all_to_all(sent, "zl", 0, 0, tiled=True)
    proj = jnp.sum(got.astype(jnp.float32), axis=0)

    lanes = -(-2 * hid // 128) * 128
    fac = local_call(
        functools.partial(factors_kernel, nx, hid, cut),
        jax.ShapeDtypeStruct((share, nx * lanes), jnp.bfloat16),
        32 * share * nx * hid,
        8 * share * columns,
        interpret,
        proj,
        in_specs=[VMEM],
        out_specs=VMEM,
    )
    fac = lax.all_gather(fac, ("zl", "c"), axis=1, tiled=True)

    away, mine = local_call(
        functools.partial(hvp_kernel, nzl, nc),
        (
            jax.ShapeDtypeStruct((nx, 2 * hid, feats), jnp.bfloat16),
            jax.ShapeDtypeStruct((2 * hid, feats), jnp.float32),
        ),
        4 * nx * hid * nc * count * feats,
        2 * nc * count * feats,
        interpret,
        x.reshape(1),
        fac,
        tok_all,
        in_specs=[SMEM, VMEM, VMEM],
        out_specs=(VMEM, VMEM),
    )
    away = lax.all_to_all(away, "x", 0, 0, tiled=True)
    diag = jax.ShapeDtypeStruct((hid, feats), jnp.float32)
    return local_call(
        functools.partial(sum_kernel, total),
        (diag, diag),
        2 * nx * hid * feats,
        8 * nx * hid * feats,
        interpret,
        x.reshape(1),
        away,
        mine,
        gate_probe,
        up_probe,
        in_specs=[SMEM] + [VMEM] * 4,
        out_specs=(VMEM, VMEM),
    )


def solution(mesh, interpret=False):
    sizes = {**NODE, **LOCAL}
    cut = Mesh(mesh.devices.reshape(tuple(sizes.values())), tuple(sizes))
    placed = P(tuple(NODE), tuple(LOCAL))
    return jax.shard_map(
        functools.partial(on_device, interpret=interpret),
        mesh=cut,
        in_specs=(placed,) * 7,
        out_specs=(placed, placed),
        check_vma=False,
    )
```

```python
import functools

import jax
import jax.numpy as jnp
from jax import lax
from jax.experimental import pallas as pl
from jax.experimental.pallas import tpu as pltpu
from jax.sharding import Mesh, PartitionSpec as P

NODE = {"zh": 2, "x": 4, "y": 8}
LOCAL = {"zl": 4, "c": 2}

PRE_SCALE = 64.0
TAN_SCALE = 0.5
BACK_SCALE = 32.0

VMEM = pl.BlockSpec(memory_space=pltpu.VMEM)
ANY = pl.BlockSpec(memory_space=pl.ANY)
SMEM = pl.BlockSpec(memory_space=pltpu.SMEM)


def swap(value, axis):
    return lax.ppermute(value, axis, [(0, 1), (1, 0)])


def shift(value, axis, by):
    size = lax.axis_size(axis)
    return lax.ppermute(value, axis, [(i, (i + by) % size) for i in range(size)])


def mix(value, axis, by):
    return lax.ppermute(value, axis, [(i, i ^ by) for i in range(lax.axis_size(axis))])


def local_call(body, out_shape, flops, moved, interpret, *args, **options):
    return pl.pallas_call(
        body,
        out_shape=out_shape,
        cost_estimate=pl.CostEstimate(flops=flops, bytes_accessed=moved, transcendentals=0),
        compiler_params=pltpu.CompilerParams(vmem_limit_bytes=16 * 1024 * 1024),
        interpret=interpret,
        **options,
    )(*args)


def pass_kernel(value, *rest):
    pass


def after(value, others, interpret):
    return local_call(
        pass_kernel,
        jax.ShapeDtypeStruct(value.shape, value.dtype),
        0,
        0,
        interpret,
        value,
        *others,
        in_specs=[ANY] * (1 + len(others)),
        out_specs=ANY,
        input_output_aliases={0: 0},
    )


def terms_kernel(tok_rows, place, tokens, cotangents, *refs):
    *weights, out, w_all = refs
    cut = len(weights) * tok_rows
    cot_rows = weights[0].shape[0] - tok_rows
    for i, weight in enumerate(weights):
        w_all[i * tok_rows : (i + 1) * tok_rows] = weight[:tok_rows]
        start = cut + i * cot_rows
        w_all[start : start + cot_rows] = weight[tok_rows:]
    count = out.shape[0]
    half = pl.ds(pl.multiple_of(place[0] * count, count), count)
    across = (((1,), (1,)), ((), ()))
    column = lax.rem(lax.broadcasted_iota(jnp.int32, (1, cut), 1), tok_rows)
    out[:, :cut] = lax.dot_general(
        tokens[half], w_all[:cut], across, preferred_element_type=jnp.float32
    ) * jnp.where(column * 2 >= tok_rows, TAN_SCALE, PRE_SCALE)
    out[:, cut:] = BACK_SCALE * lax.dot_general(
        cotangents[half], w_all[cut:], across, preferred_element_type=jnp.float32
    )


def hvp_kernel(nzl, nc, place, fac, tokens, away, own):
    nx, width, _ = away.shape
    lanes = fac.shape[1] // (nzl * nc * nx)
    for i in range(nx):
        step = place[0] ^ i
        step = step ^ (step >> 1)
        parts = []
        for c in range(nc):
            for z in range(nzl):
                start = pl.multiple_of(((z * nc + c) * nx + step) * lanes, lanes)
                parts.append(fac[:, pl.ds(start, lanes)])
        term = lax.dot_general(
            jnp.concatenate(parts, axis=0), tokens[...], (((0,), (0,)), ((), ())),
            preferred_element_type=jnp.float32,
        )[:width]
        away[i] = term.astype(away.dtype)

        @pl.when(place[0] == i)
        def _():
            own[...] = term


def sum_kernel(total, place, away, own, gate_probe, up_probe, gate_diag, up_diag):
    both = own[...]
    for i in range(away.shape[0]):
        both += jnp.where(place[0] == i, 0.0, away[i].astype(jnp.float32))
    both = both / total
    hid = gate_diag.shape[0]
    gate_diag[...] = gate_probe[...].astype(jnp.float32) * both[:hid]
    up_diag[...] = up_probe[...].astype(jnp.float32) * both[hid:]


def factors(pre_gate, pre_up, tan_gate, tan_up, back):
    sig = jax.nn.sigmoid(pre_gate)
    slope = sig * (1.0 + pre_gate * (1.0 - sig))
    bend = sig * (1.0 - sig) * (2.0 + pre_gate * (1.0 - 2.0 * sig))
    fac_gate = (back * (tan_up * slope + pre_up * bend * tan_gate)).astype(jnp.bfloat16)
    fac_up = (back * slope * tan_gate).astype(jnp.bfloat16)
    return (fac_gate, fac_up)


def factors_kernel(nx, hid, cut, proj, out):
    tok_rows, cot_rows = cut // nx, (proj.shape[1] - cut) // nx
    lanes = out.shape[1] // nx
    for i in range(nx):
        start = i * tok_rows
        pre_gate, pre_up, tan_gate, tan_up = (
            proj[:, start + j * hid : start + (j + 1) * hid] for j in range(4)
        )
        start = cut + i * cot_rows
        fac_gate, fac_up = factors(
            pre_gate * (1.0 / PRE_SCALE),
            pre_up * (1.0 / PRE_SCALE),
            tan_gate * (1.0 / TAN_SCALE),
            tan_up * (1.0 / TAN_SCALE),
            proj[:, start : start + hid] * (1.0 / BACK_SCALE),
        )
        rest = jnp.zeros((out.shape[0], lanes - 2 * hid), jnp.bfloat16)
        out[:, i * lanes : (i + 1) * lanes] = jnp.concatenate([fac_gate, fac_up, rest], axis=1)


def stacked(parts, rows):
    row, out = 0, None
    for part in parts:
        padded = lax.pad(
            part, jnp.zeros((), part.dtype),
            ((row, rows - row - part.shape[0], 0), (0, 0, 0)),
        )
        out = padded if out is None else out + padded
        row += part.shape[0]
    return out


def on_device(
    tokens, cotangent, gate_weight, up_weight, down_weight, gate_probe, up_probe, interpret
):
    nx, ny, nzl = lax.axis_size("x"), lax.axis_size("y"), lax.axis_size("zl")
    own, feats = tokens.shape
    hid = gate_weight.shape[0]
    total = own * lax.axis_size(("zh", "x", "y"))
    nc = lax.axis_size("c")
    x, core = lax.axis_index("x"), lax.axis_index("c")

    rows = stacked([tokens, cotangent], 2 * own)
    block = jnp.stack([rows, swap(rows, "zh")], axis=0)

    tok_rows, cot_rows = 4 * hid, hid * 8 // 7
    mats = stacked(
        [gate_weight, up_weight, gate_probe, up_probe, down_weight], tok_rows + cot_rows
    )
    weights = [mats] + [mix(mats, "x", by) for by in (1, 3, 2)]

    block = after(block, [mats], interpret)
    ahead = behind = block
    blocks = [block]
    for _ in range(ny // 2 - 1):
        ahead, behind = shift(ahead, "y", 1), shift(behind, "y", -1)
        blocks += [ahead, behind]
    blocks += [shift(ahead[:1], "y", 1), shift(behind[1:], "y", -1)]
    tok_all = jnp.concatenate([b[:, :own] for b in blocks], axis=0).reshape(-1, feats)
    cot_all = jnp.concatenate([b[:, own:] for b in blocks], axis=0).reshape(-1, feats)

    count = tok_all.shape[0] // nc
    cut, columns = nx * tok_rows, nx * (tok_rows + cot_rows)
    def term(which):
        return local_call(
            functools.partial(terms_kernel, tok_rows),
            jax.ShapeDtypeStruct((count, columns), jnp.float32),
            2 * count * columns * feats,
            2 * columns * feats,
            interpret,
            which.reshape(1),
            tok_all,
            cot_all,
            *weights,
            in_specs=[SMEM] + [VMEM] * (2 + nx),
            out_specs=VMEM,
            scratch_shapes=[pltpu.VMEM((columns, feats), jnp.bfloat16)],
        )
    other = swap(term(1 - core), "c")
    terms = term(core) + other

    share = count // nzl
    sent = terms.astype(jnp.float16).reshape(nzl, share, columns)
    got = lax.all_to_all(sent, "zl", 0, 0, tiled=True)
    proj = jnp.sum(got.astype(jnp.float32), axis=0)

    lanes = -(-2 * hid // 128) * 128
    fac = local_call(
        functools.partial(factors_kernel, nx, hid, cut),
        jax.ShapeDtypeStruct((share, nx * lanes), jnp.bfloat16),
        32 * share * nx * hid,
        8 * share * columns,
        interpret,
        proj,
        in_specs=[VMEM],
        out_specs=VMEM,
    )
    fac = lax.all_gather(fac, ("zl", "c"), axis=1, tiled=True)

    away, mine = local_call(
        functools.partial(hvp_kernel, nzl, nc),
        (
            jax.ShapeDtypeStruct((nx, 2 * hid, feats), jnp.bfloat16),
            jax.ShapeDtypeStruct((2 * hid, feats), jnp.float32),
        ),
        4 * nx * hid * nc * count * feats,
        2 * nc * count * feats,
        interpret,
        x.reshape(1),
        fac,
        tok_all,
        in_specs=[SMEM, VMEM, VMEM],
        out_specs=(VMEM, VMEM),
    )
    away = lax.all_to_all(away, "x", 0, 0, tiled=True)
    diag = jax.ShapeDtypeStruct((hid, feats), jnp.float32)
    return local_call(
        functools.partial(sum_kernel, total),
        (diag, diag),
        2 * nx * hid * feats,
        8 * nx * hid * feats,
        interpret,
        x.reshape(1),
        away,
        mine,
        gate_probe,
        up_probe,
        in_specs=[SMEM] + [VMEM] * 4,
        out_specs=(VMEM, VMEM),
    )


def solution(mesh, interpret=False):
    sizes = {**NODE, **LOCAL}
    cut = Mesh(mesh.devices.reshape(tuple(sizes.values())), tuple(sizes))
    placed = P(tuple(NODE), tuple(LOCAL))
    return jax.shard_map(
        functools.partial(on_device, interpret=interpret),
        mesh=cut,
        in_specs=(placed,) * 7,
        out_specs=(placed, placed),
        check_vma=False,
    )
```

```python
import functools

import jax
import jax.numpy as jnp
from jax import lax
from jax.experimental import pallas as pl
from jax.experimental.pallas import tpu as pltpu
from jax.sharding import Mesh, PartitionSpec as P

NODE = {"zh": 2, "x": 4, "y": 8}
LOCAL = {"zl": 4, "c": 2}

PRE_SCALE = 64.0
TAN_SCALE = 0.5
BACK_SCALE = 32.0

VMEM = pl.BlockSpec(memory_space=pltpu.VMEM)
ANY = pl.BlockSpec(memory_space=pl.ANY)
SMEM = pl.BlockSpec(memory_space=pltpu.SMEM)


def swap(value, axis):
    return lax.ppermute(value, axis, [(0, 1), (1, 0)])


def shift(value, axis, by):
    size = lax.axis_size(axis)
    return lax.ppermute(value, axis, [(i, (i + by) % size) for i in range(size)])


def mix(value, axis, by):
    return lax.ppermute(value, axis, [(i, i ^ by) for i in range(lax.axis_size(axis))])


def local_call(body, out_shape, flops, moved, interpret, *args, **options):
    return pl.pallas_call(
        body,
        out_shape=out_shape,
        cost_estimate=pl.CostEstimate(flops=flops, bytes_accessed=moved, transcendentals=0),
        compiler_params=pltpu.CompilerParams(vmem_limit_bytes=16 * 1024 * 1024),
        interpret=interpret,
        **options,
    )(*args)


def pass_kernel(value, *rest):
    pass


def after(value, others, interpret):
    return local_call(
        pass_kernel,
        jax.ShapeDtypeStruct(value.shape, value.dtype),
        0,
        0,
        interpret,
        value,
        *others,
        in_specs=[ANY] * (1 + len(others)),
        out_specs=ANY,
        input_output_aliases={0: 0},
    )


def terms_kernel(tok_rows, place, tokens, cotangents, *refs):
    *weights, out, w_all = refs
    cut = len(weights) * tok_rows
    cot_rows = weights[0].shape[0] - tok_rows
    for i, weight in enumerate(weights):
        w_all[i * tok_rows : (i + 1) * tok_rows] = weight[:tok_rows]
        start = cut + i * cot_rows
        w_all[start : start + cot_rows] = weight[tok_rows:]
    count = out.shape[0]
    half = pl.ds(pl.multiple_of(place[0] * count, count), count)
    across = (((1,), (1,)), ((), ()))
    column = lax.rem(lax.broadcasted_iota(jnp.int32, (1, cut), 1), tok_rows)
    out[:, :cut] = lax.dot_general(
        tokens[half], w_all[:cut], across, preferred_element_type=jnp.float32
    ) * jnp.where(column * 2 >= tok_rows, TAN_SCALE, PRE_SCALE)
    out[:, cut:] = BACK_SCALE * lax.dot_general(
        cotangents[half], w_all[cut:], across, preferred_element_type=jnp.float32
    )


def hvp_kernel(nzl, nc, place, fac, tokens, away, own):
    nx, width, _ = away.shape
    lanes = fac.shape[1] // (nzl * nc * nx)
    for i in range(nx):
        step = place[0] ^ i
        step = step ^ (step >> 1)
        parts = []
        for c in range(nc):
            for z in range(nzl):
                start = pl.multiple_of(((z * nc + c) * nx + step) * lanes, lanes)
                parts.append(fac[:, pl.ds(start, lanes)])
        term = lax.dot_general(
            jnp.concatenate(parts, axis=0), tokens[...], (((0,), (0,)), ((), ())),
            preferred_element_type=jnp.float32,
        )[:width]
        away[i] = term.astype(away.dtype)

        @pl.when(place[0] == i)
        def _():
            own[...] = term


def sum_kernel(total, place, away, own, gate_probe, up_probe, gate_diag, up_diag):
    both = own[...]
    for i in range(away.shape[0]):
        both += jnp.where(place[0] == i, 0.0, away[i].astype(jnp.float32))
    both = both / total
    hid = gate_diag.shape[0]
    gate_diag[...] = gate_probe[...].astype(jnp.float32) * both[:hid]
    up_diag[...] = up_probe[...].astype(jnp.float32) * both[hid:]


def factors(pre_gate, pre_up, tan_gate, tan_up, back):
    sig = jax.nn.sigmoid(pre_gate)
    slope = sig * (1.0 + pre_gate * (1.0 - sig))
    bend = sig * (1.0 - sig) * (2.0 + pre_gate * (1.0 - 2.0 * sig))
    fac_gate = (back * (tan_up * slope + pre_up * bend * tan_gate)).astype(jnp.bfloat16)
    fac_up = (back * slope * tan_gate).astype(jnp.bfloat16)
    return (fac_gate, fac_up)


def factors_kernel(nx, hid, cut, proj, out):
    tok_rows, cot_rows = cut // nx, (proj.shape[1] - cut) // nx
    lanes = out.shape[1] // nx
    for i in range(nx):
        start = i * tok_rows
        pre_gate, pre_up, tan_gate, tan_up = (
            proj[:, start + j * hid : start + (j + 1) * hid] for j in range(4)
        )
        start = cut + i * cot_rows
        fac_gate, fac_up = factors(
            pre_gate * (1.0 / PRE_SCALE),
            pre_up * (1.0 / PRE_SCALE),
            tan_gate * (1.0 / TAN_SCALE),
            tan_up * (1.0 / TAN_SCALE),
            proj[:, start : start + hid] * (1.0 / BACK_SCALE),
        )
        rest = jnp.zeros((out.shape[0], lanes - 2 * hid), jnp.bfloat16)
        out[:, i * lanes : (i + 1) * lanes] = jnp.concatenate([fac_gate, fac_up, rest], axis=1)


def stacked(parts, rows):
    row, out = 0, None
    for part in parts:
        padded = lax.pad(
            part, jnp.zeros((), part.dtype),
            ((row, rows - row - part.shape[0], 0), (0, 0, 0)),
        )
        out = padded if out is None else out + padded
        row += part.shape[0]
    return out


def on_device(
    tokens, cotangent, gate_weight, up_weight, down_weight, gate_probe, up_probe, interpret
):
    nx, ny, nzl = lax.axis_size("x"), lax.axis_size("y"), lax.axis_size("zl")
    own, feats = tokens.shape
    hid = gate_weight.shape[0]
    total = own * lax.axis_size(("zh", "x", "y"))
    nc = lax.axis_size("c")
    x, core = lax.axis_index("x"), lax.axis_index("c")

    rows = stacked([tokens, cotangent], 2 * own)
    block = jnp.stack([rows, swap(rows, "zh")], axis=0)

    tok_rows, cot_rows = 4 * hid, hid * 8 // 7
    mats = stacked(
        [gate_weight, up_weight, gate_probe, up_probe, down_weight], tok_rows + cot_rows
    )
    weights = [mats] + [mix(mats, "x", by) for by in (1, 3, 2)]

    ahead = behind = block
    blocks = [block]
    for step in range(ny // 2 - 1):
        if step == 1:
            ahead = after(ahead, weights[1:2], interpret)
        ahead, behind = shift(ahead, "y", 1), shift(behind, "y", -1)
        blocks += [ahead, behind]
    blocks += [shift(ahead[:1], "y", 1), shift(behind[1:], "y", -1)]
    tok_all = jnp.concatenate([b[:, :own] for b in blocks], axis=0).reshape(-1, feats)
    cot_all = jnp.concatenate([b[:, own:] for b in blocks], axis=0).reshape(-1, feats)

    count = tok_all.shape[0] // nc
    cut, columns = nx * tok_rows, nx * (tok_rows + cot_rows)
    def term(which):
        return local_call(
            functools.partial(terms_kernel, tok_rows),
            jax.ShapeDtypeStruct((count, columns), jnp.float32),
            2 * count * columns * feats,
            2 * columns * feats,
            interpret,
            which.reshape(1),
            tok_all,
            cot_all,
            *weights,
            in_specs=[SMEM] + [VMEM] * (2 + nx),
            out_specs=VMEM,
            scratch_shapes=[pltpu.VMEM((columns, feats), jnp.bfloat16)],
        )
    other = swap(term(1 - core), "c")
    terms = term(core) + other

    share = count // nzl
    sent = terms.astype(jnp.float16).reshape(nzl, share, columns)
    got = lax.all_to_all(sent, "zl", 0, 0, tiled=True)
    proj = jnp.sum(got.astype(jnp.float32), axis=0)

    lanes = -(-2 * hid // 128) * 128
    fac = local_call(
        functools.partial(factors_kernel, nx, hid, cut),
        jax.ShapeDtypeStruct((share, nx * lanes), jnp.bfloat16),
        32 * share * nx * hid,
        8 * share * columns,
        interpret,
        proj,
        in_specs=[VMEM],
        out_specs=VMEM,
    )
    fac = lax.all_gather(fac, ("zl", "c"), axis=1, tiled=True)

    away, mine = local_call(
        functools.partial(hvp_kernel, nzl, nc),
        (
            jax.ShapeDtypeStruct((nx, 2 * hid, feats), jnp.bfloat16),
            jax.ShapeDtypeStruct((2 * hid, feats), jnp.float32),
        ),
        4 * nx * hid * nc * count * feats,
        2 * nc * count * feats,
        interpret,
        x.reshape(1),
        fac,
        tok_all,
        in_specs=[SMEM, VMEM, VMEM],
        out_specs=(VMEM, VMEM),
    )
    away = lax.all_to_all(away, "x", 0, 0, tiled=True)
    diag = jax.ShapeDtypeStruct((hid, feats), jnp.float32)
    return local_call(
        functools.partial(sum_kernel, total),
        (diag, diag),
        2 * nx * hid * feats,
        8 * nx * hid * feats,
        interpret,
        x.reshape(1),
        away,
        mine,
        gate_probe,
        up_probe,
        in_specs=[SMEM] + [VMEM] * 4,
        out_specs=(VMEM, VMEM),
    )


def solution(mesh, interpret=False):
    sizes = {**NODE, **LOCAL}
    cut = Mesh(mesh.devices.reshape(tuple(sizes.values())), tuple(sizes))
    placed = P(tuple(NODE), tuple(LOCAL))
    return jax.shard_map(
        functools.partial(on_device, interpret=interpret),
        mesh=cut,
        in_specs=(placed,) * 7,
        out_specs=(placed, placed),
        check_vma=False,
    )
```

```python
import functools

import jax
import jax.numpy as jnp
from jax import lax
from jax.experimental import pallas as pl
from jax.experimental.pallas import tpu as pltpu
from jax.sharding import Mesh, PartitionSpec as P

NODE = {"zh": 2, "x": 4, "y": 8}
LOCAL = {"zl": 4, "c": 2}

PRE_SCALE = 64.0
TAN_SCALE = 0.5
BACK_SCALE = 32.0

VMEM = pl.BlockSpec(memory_space=pltpu.VMEM)
ANY = pl.BlockSpec(memory_space=pl.ANY)
SMEM = pl.BlockSpec(memory_space=pltpu.SMEM)


def swap(value, axis):
    return lax.ppermute(value, axis, [(0, 1), (1, 0)])


def shift(value, axis, by):
    size = lax.axis_size(axis)
    return lax.ppermute(value, axis, [(i, (i + by) % size) for i in range(size)])


def mix(value, axis, by):
    return lax.ppermute(value, axis, [(i, i ^ by) for i in range(lax.axis_size(axis))])


def local_call(body, out_shape, flops, moved, interpret, *args, **options):
    return pl.pallas_call(
        body,
        out_shape=out_shape,
        cost_estimate=pl.CostEstimate(flops=flops, bytes_accessed=moved, transcendentals=0),
        compiler_params=pltpu.CompilerParams(vmem_limit_bytes=16 * 1024 * 1024),
        interpret=interpret,
        **options,
    )(*args)


def pass_kernel(value, *rest):
    pass


def after(value, others, interpret):
    return local_call(
        pass_kernel,
        jax.ShapeDtypeStruct(value.shape, value.dtype),
        0,
        0,
        interpret,
        value,
        *others,
        in_specs=[ANY] * (1 + len(others)),
        out_specs=ANY,
        input_output_aliases={0: 0},
    )


def terms_kernel(tok_rows, place, tokens, cotangents, *refs):
    *weights, out, w_all = refs
    cut = len(weights) * tok_rows
    cot_rows = weights[0].shape[0] - tok_rows
    for i, weight in enumerate(weights):
        w_all[i * tok_rows : (i + 1) * tok_rows] = weight[:tok_rows]
        start = cut + i * cot_rows
        w_all[start : start + cot_rows] = weight[tok_rows:]
    count = out.shape[0]
    half = pl.ds(pl.multiple_of(place[0] * count, count), count)
    across = (((1,), (1,)), ((), ()))
    column = lax.rem(lax.broadcasted_iota(jnp.int32, (1, cut), 1), tok_rows)
    out[:, :cut] = lax.dot_general(
        tokens[half], w_all[:cut], across, preferred_element_type=jnp.float32
    ) * jnp.where(column * 2 >= tok_rows, TAN_SCALE, PRE_SCALE)
    out[:, cut:] = BACK_SCALE * lax.dot_general(
        cotangents[half], w_all[cut:], across, preferred_element_type=jnp.float32
    )


def hvp_kernel(nzl, nc, place, fac, tokens, away, own):
    nx, width, _ = away.shape
    lanes = fac.shape[1] // (nzl * nc * nx)
    for i in range(nx):
        step = place[0] ^ i
        step = step ^ (step >> 1)
        parts = []
        for c in range(nc):
            for z in range(nzl):
                start = pl.multiple_of(((z * nc + c) * nx + step) * lanes, lanes)
                parts.append(fac[:, pl.ds(start, lanes)])
        term = lax.dot_general(
            jnp.concatenate(parts, axis=0), tokens[...], (((0,), (0,)), ((), ())),
            preferred_element_type=jnp.float32,
        )[:width]
        away[i] = term.astype(away.dtype)

        @pl.when(place[0] == i)
        def _():
            own[...] = term


def sum_kernel(total, place, away, own, gate_probe, up_probe, gate_diag, up_diag):
    both = own[...]
    for i in range(away.shape[0]):
        both += jnp.where(place[0] == i, 0.0, away[i].astype(jnp.float32))
    both = both / total
    hid = gate_diag.shape[0]
    gate_diag[...] = gate_probe[...].astype(jnp.float32) * both[:hid]
    up_diag[...] = up_probe[...].astype(jnp.float32) * both[hid:]


def factors(pre_gate, pre_up, tan_gate, tan_up, back):
    sig = jax.nn.sigmoid(pre_gate)
    slope = sig * (1.0 + pre_gate * (1.0 - sig))
    bend = sig * (1.0 - sig) * (2.0 + pre_gate * (1.0 - 2.0 * sig))
    fac_gate = (back * (tan_up * slope + pre_up * bend * tan_gate)).astype(jnp.bfloat16)
    fac_up = (back * slope * tan_gate).astype(jnp.bfloat16)
    return (fac_gate, fac_up)


def factors_kernel(nx, hid, cut, proj, out):
    tok_rows, cot_rows = cut // nx, (proj.shape[1] - cut) // nx
    lanes = out.shape[1] // nx
    for i in range(nx):
        start = i * tok_rows
        pre_gate, pre_up, tan_gate, tan_up = (
            proj[:, start + j * hid : start + (j + 1) * hid] for j in range(4)
        )
        start = cut + i * cot_rows
        fac_gate, fac_up = factors(
            pre_gate * (1.0 / PRE_SCALE),
            pre_up * (1.0 / PRE_SCALE),
            tan_gate * (1.0 / TAN_SCALE),
            tan_up * (1.0 / TAN_SCALE),
            proj[:, start : start + hid] * (1.0 / BACK_SCALE),
        )
        rest = jnp.zeros((out.shape[0], lanes - 2 * hid), jnp.bfloat16)
        out[:, i * lanes : (i + 1) * lanes] = jnp.concatenate([fac_gate, fac_up, rest], axis=1)


def stacked(parts, rows):
    row, out = 0, None
    for part in parts:
        padded = lax.pad(
            part, jnp.zeros((), part.dtype),
            ((row, rows - row - part.shape[0], 0), (0, 0, 0)),
        )
        out = padded if out is None else out + padded
        row += part.shape[0]
    return out


def on_device(
    tokens, cotangent, gate_weight, up_weight, down_weight, gate_probe, up_probe, interpret
):
    nx, ny, nzl = lax.axis_size("x"), lax.axis_size("y"), lax.axis_size("zl")
    own, feats = tokens.shape
    hid = gate_weight.shape[0]
    total = own * lax.axis_size(("zh", "x", "y"))
    nc = lax.axis_size("c")
    x, core = lax.axis_index("x"), lax.axis_index("c")

    rows = stacked([tokens, cotangent], 2 * own)
    block = jnp.stack([rows, swap(rows, "zh")], axis=0)

    tok_rows, cot_rows = 4 * hid, hid * 8 // 7
    mats = stacked(
        [gate_weight, up_weight, gate_probe, up_probe, down_weight], tok_rows + cot_rows
    )
    beside, across = mix(mats, "x", 1), mix(mats, "x", 3)

    block = after(block, [mats], interpret)
    ahead = behind = block
    blocks = [block]
    for step in range(ny // 2 - 1):
        ahead, behind = shift(ahead, "y", 1), shift(behind, "y", -1)
        if step == 1:
            beside = after(beside, [ahead], interpret)
        blocks += [ahead, behind]
    blocks += [shift(ahead[:1], "y", 1), shift(behind[1:], "y", -1)]
    weights = [mats, beside, across, mix(beside, "x", 3)]
    tok_all = jnp.concatenate([b[:, :own] for b in blocks], axis=0).reshape(-1, feats)
    cot_all = jnp.concatenate([b[:, own:] for b in blocks], axis=0).reshape(-1, feats)

    count = tok_all.shape[0] // nc
    cut, columns = nx * tok_rows, nx * (tok_rows + cot_rows)
    def term(which):
        return local_call(
            functools.partial(terms_kernel, tok_rows),
            jax.ShapeDtypeStruct((count, columns), jnp.float32),
            2 * count * columns * feats,
            2 * columns * feats,
            interpret,
            which.reshape(1),
            tok_all,
            cot_all,
            *weights,
            in_specs=[SMEM] + [VMEM] * (2 + nx),
            out_specs=VMEM,
            scratch_shapes=[pltpu.VMEM((columns, feats), jnp.bfloat16)],
        )
    other = swap(term(1 - core), "c")
    terms = term(core) + other

    share = count // nzl
    sent = terms.astype(jnp.float16).reshape(nzl, share, columns)
    got = lax.all_to_all(sent, "zl", 0, 0, tiled=True)
    proj = jnp.sum(got.astype(jnp.float32), axis=0)

    lanes = -(-2 * hid // 128) * 128
    fac = local_call(
        functools.partial(factors_kernel, nx, hid, cut),
        jax.ShapeDtypeStruct((share, nx * lanes), jnp.bfloat16),
        32 * share * nx * hid,
        8 * share * columns,
        interpret,
        proj,
        in_specs=[VMEM],
        out_specs=VMEM,
    )
    fac = lax.all_gather(fac, ("zl", "c"), axis=1, tiled=True)

    away, mine = local_call(
        functools.partial(hvp_kernel, nzl, nc),
        (
            jax.ShapeDtypeStruct((nx, 2 * hid, feats), jnp.bfloat16),
            jax.ShapeDtypeStruct((2 * hid, feats), jnp.float32),
        ),
        4 * nx * hid * nc * count * feats,
        2 * nc * count * feats,
        interpret,
        x.reshape(1),
        fac,
        tok_all,
        in_specs=[SMEM, VMEM, VMEM],
        out_specs=(VMEM, VMEM),
    )
    away = lax.all_to_all(away, "x", 0, 0, tiled=True)
    diag = jax.ShapeDtypeStruct((hid, feats), jnp.float32)
    return local_call(
        functools.partial(sum_kernel, total),
        (diag, diag),
        2 * nx * hid * feats,
        8 * nx * hid * feats,
        interpret,
        x.reshape(1),
        away,
        mine,
        gate_probe,
        up_probe,
        in_specs=[SMEM] + [VMEM] * 4,
        out_specs=(VMEM, VMEM),
    )


def solution(mesh, interpret=False):
    sizes = {**NODE, **LOCAL}
    cut = Mesh(mesh.devices.reshape(tuple(sizes.values())), tuple(sizes))
    placed = P(tuple(NODE), tuple(LOCAL))
    return jax.shard_map(
        functools.partial(on_device, interpret=interpret),
        mesh=cut,
        in_specs=(placed,) * 7,
        out_specs=(placed, placed),
        check_vma=False,
    )
```

```python
import functools

import jax
import jax.numpy as jnp
from jax import lax
from jax.experimental import pallas as pl
from jax.experimental.pallas import tpu as pltpu
from jax.sharding import Mesh, PartitionSpec as P

NODE = {"zh": 2, "x": 4, "y": 8}
LOCAL = {"zl": 4, "c": 2}

PRE_SCALE = 64.0
TAN_SCALE = 0.5
BACK_SCALE = 32.0

VMEM = pl.BlockSpec(memory_space=pltpu.VMEM)
ANY = pl.BlockSpec(memory_space=pl.ANY)
SMEM = pl.BlockSpec(memory_space=pltpu.SMEM)


def swap(value, axis):
    return lax.ppermute(value, axis, [(0, 1), (1, 0)])


def shift(value, axis, by):
    size = lax.axis_size(axis)
    return lax.ppermute(value, axis, [(i, (i + by) % size) for i in range(size)])


def mix(value, axis, by):
    return lax.ppermute(value, axis, [(i, i ^ by) for i in range(lax.axis_size(axis))])


def local_call(body, out_shape, flops, moved, interpret, *args, **options):
    return pl.pallas_call(
        body,
        out_shape=out_shape,
        cost_estimate=pl.CostEstimate(flops=flops, bytes_accessed=moved, transcendentals=0),
        compiler_params=pltpu.CompilerParams(vmem_limit_bytes=16 * 1024 * 1024),
        interpret=interpret,
        **options,
    )(*args)


def pass_kernel(value, *rest):
    pass


def after(value, others, interpret):
    return local_call(
        pass_kernel,
        jax.ShapeDtypeStruct(value.shape, value.dtype),
        0,
        0,
        interpret,
        value,
        *others,
        in_specs=[ANY] * (1 + len(others)),
        out_specs=ANY,
        input_output_aliases={0: 0},
    )


def terms_kernel(tok_rows, place, tokens, cotangents, *refs):
    *weights, out, w_all = refs
    cut = len(weights) * tok_rows
    cot_rows = weights[0].shape[0] - tok_rows
    for i, weight in enumerate(weights):
        w_all[i * tok_rows : (i + 1) * tok_rows] = weight[:tok_rows]
        start = cut + i * cot_rows
        w_all[start : start + cot_rows] = weight[tok_rows:]
    count = out.shape[0]
    half = pl.ds(pl.multiple_of(place[0] * count, count), count)
    across = (((1,), (1,)), ((), ()))
    column = lax.rem(lax.broadcasted_iota(jnp.int32, (1, cut), 1), tok_rows)
    out[:, :cut] = lax.dot_general(
        tokens[half], w_all[:cut], across, preferred_element_type=jnp.float32
    ) * jnp.where(column * 2 >= tok_rows, TAN_SCALE, PRE_SCALE)
    out[:, cut:] = BACK_SCALE * lax.dot_general(
        cotangents[half], w_all[cut:], across, preferred_element_type=jnp.float32
    )


def hvp_kernel(nzl, nc, place, fac, tokens, away, own):
    nx, width, _ = away.shape
    lanes = fac.shape[1] // (nzl * nc * nx)
    for i in range(nx):
        step = place[0] ^ i
        step = step ^ (step >> 1)
        parts = []
        for c in range(nc):
            for z in range(nzl):
                start = pl.multiple_of(((z * nc + c) * nx + step) * lanes, lanes)
                parts.append(fac[:, pl.ds(start, lanes)])
        term = lax.dot_general(
            jnp.concatenate(parts, axis=0), tokens[...], (((0,), (0,)), ((), ())),
            preferred_element_type=jnp.float32,
        )[:width]
        away[i] = term.astype(away.dtype)

        @pl.when(place[0] == i)
        def _():
            own[...] = term


def sum_kernel(total, place, away, own, gate_probe, up_probe, gate_diag, up_diag):
    both = own[...]
    for i in range(away.shape[0]):
        both += jnp.where(place[0] == i, 0.0, away[i].astype(jnp.float32))
    both = both / total
    hid = gate_diag.shape[0]
    gate_diag[...] = gate_probe[...].astype(jnp.float32) * both[:hid]
    up_diag[...] = up_probe[...].astype(jnp.float32) * both[hid:]


def factors(pre_gate, pre_up, tan_gate, tan_up, back):
    sig = jax.nn.sigmoid(pre_gate)
    slope = sig * (1.0 + pre_gate * (1.0 - sig))
    bend = sig * (1.0 - sig) * (2.0 + pre_gate * (1.0 - 2.0 * sig))
    fac_gate = (back * (tan_up * slope + pre_up * bend * tan_gate)).astype(jnp.bfloat16)
    fac_up = (back * slope * tan_gate).astype(jnp.bfloat16)
    return (fac_gate, fac_up)


def factors_kernel(nx, hid, cut, proj, out):
    tok_rows, cot_rows = cut // nx, (proj.shape[1] - cut) // nx
    lanes = out.shape[1] // nx
    for i in range(nx):
        start = i * tok_rows
        pre_gate, pre_up, tan_gate, tan_up = (
            proj[:, start + j * hid : start + (j + 1) * hid] for j in range(4)
        )
        start = cut + i * cot_rows
        fac_gate, fac_up = factors(
            pre_gate * (1.0 / PRE_SCALE),
            pre_up * (1.0 / PRE_SCALE),
            tan_gate * (1.0 / TAN_SCALE),
            tan_up * (1.0 / TAN_SCALE),
            proj[:, start : start + hid] * (1.0 / BACK_SCALE),
        )
        rest = jnp.zeros((out.shape[0], lanes - 2 * hid), jnp.bfloat16)
        out[:, i * lanes : (i + 1) * lanes] = jnp.concatenate([fac_gate, fac_up, rest], axis=1)


def stacked(parts, rows):
    row, out = 0, None
    for part in parts:
        padded = lax.pad(
            part, jnp.zeros((), part.dtype),
            ((row, rows - row - part.shape[0], 0), (0, 0, 0)),
        )
        out = padded if out is None else out + padded
        row += part.shape[0]
    return out


def on_device(
    tokens, cotangent, gate_weight, up_weight, down_weight, gate_probe, up_probe, interpret
):
    nx, ny, nzl = lax.axis_size("x"), lax.axis_size("y"), lax.axis_size("zl")
    own, feats = tokens.shape
    hid = gate_weight.shape[0]
    total = own * lax.axis_size(("zh", "x", "y"))
    nc = lax.axis_size("c")
    x, core = lax.axis_index("x"), lax.axis_index("c")

    rows = stacked([tokens, cotangent], 2 * own)
    block = jnp.stack([rows, swap(rows, "zh")], axis=0)

    tok_rows, cot_rows = 4 * hid, hid * 8 // 7
    mats = stacked(
        [gate_weight, up_weight, gate_probe, up_probe, down_weight], tok_rows + cot_rows
    )
    beside, across = mix(mats, "x", 1), mix(mats, "x", 3)

    ahead = behind = block
    blocks = [block]
    for step in range(ny // 2 - 1):
        ahead, behind = shift(ahead, "y", 1), shift(behind, "y", -1)
        if step == 0:
            behind = after(behind, [beside], interpret)
        if step == 1:
            beside = after(beside, [ahead], interpret)
        blocks += [ahead, behind]
    blocks += [shift(ahead[:1], "y", 1), shift(behind[1:], "y", -1)]
    weights = [mats, beside, across, mix(beside, "x", 3)]
    tok_all = jnp.concatenate([b[:, :own] for b in blocks], axis=0).reshape(-1, feats)
    cot_all = jnp.concatenate([b[:, own:] for b in blocks], axis=0).reshape(-1, feats)

    count = tok_all.shape[0] // nc
    cut, columns = nx * tok_rows, nx * (tok_rows + cot_rows)
    def term(which):
        return local_call(
            functools.partial(terms_kernel, tok_rows),
            jax.ShapeDtypeStruct((count, columns), jnp.float32),
            2 * count * columns * feats,
            2 * columns * feats,
            interpret,
            which.reshape(1),
            tok_all,
            cot_all,
            *weights,
            in_specs=[SMEM] + [VMEM] * (2 + nx),
            out_specs=VMEM,
            scratch_shapes=[pltpu.VMEM((columns, feats), jnp.bfloat16)],
        )
    other = swap(term(1 - core), "c")
    terms = term(core) + other

    share = count // nzl
    sent = terms.astype(jnp.float16).reshape(nzl, share, columns)
    got = lax.all_to_all(sent, "zl", 0, 0, tiled=True)
    proj = jnp.sum(got.astype(jnp.float32), axis=0)

    lanes = -(-2 * hid // 128) * 128
    fac = local_call(
        functools.partial(factors_kernel, nx, hid, cut),
        jax.ShapeDtypeStruct((share, nx * lanes), jnp.bfloat16),
        32 * share * nx * hid,
        8 * share * columns,
        interpret,
        proj,
        in_specs=[VMEM],
        out_specs=VMEM,
    )
    fac = lax.all_gather(fac, ("zl", "c"), axis=1, tiled=True)

    away, mine = local_call(
        functools.partial(hvp_kernel, nzl, nc),
        (
            jax.ShapeDtypeStruct((nx, 2 * hid, feats), jnp.bfloat16),
            jax.ShapeDtypeStruct((2 * hid, feats), jnp.float32),
        ),
        4 * nx * hid * nc * count * feats,
        2 * nc * count * feats,
        interpret,
        x.reshape(1),
        fac,
        tok_all,
        in_specs=[SMEM, VMEM, VMEM],
        out_specs=(VMEM, VMEM),
    )
    away = lax.all_to_all(away, "x", 0, 0, tiled=True)
    diag = jax.ShapeDtypeStruct((hid, feats), jnp.float32)
    return local_call(
        functools.partial(sum_kernel, total),
        (diag, diag),
        2 * nx * hid * feats,
        8 * nx * hid * feats,
        interpret,
        x.reshape(1),
        away,
        mine,
        gate_probe,
        up_probe,
        in_specs=[SMEM] + [VMEM] * 4,
        out_specs=(VMEM, VMEM),
    )


def solution(mesh, interpret=False):
    sizes = {**NODE, **LOCAL}
    cut = Mesh(mesh.devices.reshape(tuple(sizes.values())), tuple(sizes))
    placed = P(tuple(NODE), tuple(LOCAL))
    return jax.shard_map(
        functools.partial(on_device, interpret=interpret),
        mesh=cut,
        in_specs=(placed,) * 7,
        out_specs=(placed, placed),
        check_vma=False,
    )
```

```python
import functools

import jax
import jax.numpy as jnp
from jax import lax
from jax.experimental import pallas as pl
from jax.experimental.pallas import tpu as pltpu
from jax.sharding import Mesh, PartitionSpec as P

NODE = {"zh": 2, "x": 4, "y": 8}
LOCAL = {"zl": 4, "c": 2}

PRE_SCALE = 64.0
TAN_SCALE = 0.5
BACK_SCALE = 32.0

VMEM = pl.BlockSpec(memory_space=pltpu.VMEM)
ANY = pl.BlockSpec(memory_space=pl.ANY)
SMEM = pl.BlockSpec(memory_space=pltpu.SMEM)


def swap(value, axis):
    return lax.ppermute(value, axis, [(0, 1), (1, 0)])


def shift(value, axis, by):
    size = lax.axis_size(axis)
    return lax.ppermute(value, axis, [(i, (i + by) % size) for i in range(size)])


def mix(value, axis, by):
    return lax.ppermute(value, axis, [(i, i ^ by) for i in range(lax.axis_size(axis))])


def local_call(body, out_shape, flops, moved, interpret, *args, **options):
    return pl.pallas_call(
        body,
        out_shape=out_shape,
        cost_estimate=pl.CostEstimate(flops=flops, bytes_accessed=moved, transcendentals=0),
        compiler_params=pltpu.CompilerParams(vmem_limit_bytes=16 * 1024 * 1024),
        interpret=interpret,
        **options,
    )(*args)


def pass_kernel(value, *rest):
    pass


def after(value, others, interpret):
    return local_call(
        pass_kernel,
        jax.ShapeDtypeStruct(value.shape, value.dtype),
        0,
        0,
        interpret,
        value,
        *others,
        in_specs=[ANY] * (1 + len(others)),
        out_specs=ANY,
        input_output_aliases={0: 0},
    )


def terms_kernel(tok_rows, place, tokens, cotangents, *refs):
    *weights, out, w_all = refs
    cut = len(weights) * tok_rows
    cot_rows = weights[0].shape[0] - tok_rows
    for i, weight in enumerate(weights):
        w_all[i * tok_rows : (i + 1) * tok_rows] = weight[:tok_rows]
        start = cut + i * cot_rows
        w_all[start : start + cot_rows] = weight[tok_rows:]
    count = out.shape[0]
    half = pl.ds(pl.multiple_of(place[0] * count, count), count)
    across = (((1,), (1,)), ((), ()))
    column = lax.rem(lax.broadcasted_iota(jnp.int32, (1, cut), 1), tok_rows)
    out[:, :cut] = lax.dot_general(
        tokens[half], w_all[:cut], across, preferred_element_type=jnp.float32
    ) * jnp.where(column * 2 >= tok_rows, TAN_SCALE, PRE_SCALE)
    out[:, cut:] = BACK_SCALE * lax.dot_general(
        cotangents[half], w_all[cut:], across, preferred_element_type=jnp.float32
    )


def hvp_kernel(nzl, nc, place, fac, tokens, away, own):
    nx, width, _ = away.shape
    lanes = fac.shape[1] // (nzl * nc * nx)
    for i in range(nx):
        step = place[0] ^ i
        step = step ^ (step >> 1)
        parts = []
        for c in range(nc):
            for z in range(nzl):
                start = pl.multiple_of(((z * nc + c) * nx + step) * lanes, lanes)
                parts.append(fac[:, pl.ds(start, lanes)])
        term = lax.dot_general(
            jnp.concatenate(parts, axis=0), tokens[...], (((0,), (0,)), ((), ())),
            preferred_element_type=jnp.float32,
        )[:width]
        away[i] = term.astype(away.dtype)

        @pl.when(place[0] == i)
        def _():
            own[...] = term


def sum_kernel(total, place, away, own, gate_probe, up_probe, gate_diag, up_diag):
    both = own[...]
    for i in range(away.shape[0]):
        both += jnp.where(place[0] == i, 0.0, away[i].astype(jnp.float32))
    both = both / total
    hid = gate_diag.shape[0]
    gate_diag[...] = gate_probe[...].astype(jnp.float32) * both[:hid]
    up_diag[...] = up_probe[...].astype(jnp.float32) * both[hid:]


def factors(pre_gate, pre_up, tan_gate, tan_up, back):
    sig = jax.nn.sigmoid(pre_gate)
    slope = sig * (1.0 + pre_gate * (1.0 - sig))
    bend = sig * (1.0 - sig) * (2.0 + pre_gate * (1.0 - 2.0 * sig))
    fac_gate = (back * (tan_up * slope + pre_up * bend * tan_gate)).astype(jnp.bfloat16)
    fac_up = (back * slope * tan_gate).astype(jnp.bfloat16)
    return (fac_gate, fac_up)


def factors_kernel(nx, hid, cut, proj, out):
    tok_rows, cot_rows = cut // nx, (proj.shape[1] - cut) // nx
    lanes = out.shape[1] // nx
    for i in range(nx):
        start = i * tok_rows
        pre_gate, pre_up, tan_gate, tan_up = (
            proj[:, start + j * hid : start + (j + 1) * hid] for j in range(4)
        )
        start = cut + i * cot_rows
        fac_gate, fac_up = factors(
            pre_gate * (1.0 / PRE_SCALE),
            pre_up * (1.0 / PRE_SCALE),
            tan_gate * (1.0 / TAN_SCALE),
            tan_up * (1.0 / TAN_SCALE),
            proj[:, start : start + hid] * (1.0 / BACK_SCALE),
        )
        rest = jnp.zeros((out.shape[0], lanes - 2 * hid), jnp.bfloat16)
        out[:, i * lanes : (i + 1) * lanes] = jnp.concatenate([fac_gate, fac_up, rest], axis=1)


def stacked(parts, rows):
    row, out = 0, None
    for part in parts:
        padded = lax.pad(
            part, jnp.zeros((), part.dtype),
            ((row, rows - row - part.shape[0], 0), (0, 0, 0)),
        )
        out = padded if out is None else out + padded
        row += part.shape[0]
    return out


def on_device(
    tokens, cotangent, gate_weight, up_weight, down_weight, gate_probe, up_probe, interpret
):
    nx, ny, nzl = lax.axis_size("x"), lax.axis_size("y"), lax.axis_size("zl")
    own, feats = tokens.shape
    hid = gate_weight.shape[0]
    total = own * lax.axis_size(("zh", "x", "y"))
    nc = lax.axis_size("c")
    x, core = lax.axis_index("x"), lax.axis_index("c")

    rows = stacked([tokens, cotangent], 2 * own)
    block = jnp.stack([rows, swap(rows, "zh")], axis=0)

    tok_rows, cot_rows = 4 * hid, hid * 8 // 7
    mats = stacked(
        [gate_weight, up_weight, gate_probe, up_probe, down_weight], tok_rows + cot_rows
    )
    beside, across = mix(mats, "x", 1), mix(mats, "x", 3)

    ahead = behind = block
    blocks = [block]
    for step in range(ny // 2 - 1):
        ahead, behind = shift(ahead, "y", 1), shift(behind, "y", -1)
        if step == 0:
            behind = after(behind, [beside], interpret)
        if step == 1:
            beside = after(beside, [behind], interpret)
        blocks += [ahead, behind]
    blocks += [shift(ahead[:1], "y", 1), shift(behind[1:], "y", -1)]
    weights = [mats, beside, across, mix(beside, "x", 3)]
    tok_all = jnp.concatenate([b[:, :own] for b in blocks], axis=0).reshape(-1, feats)
    cot_all = jnp.concatenate([b[:, own:] for b in blocks], axis=0).reshape(-1, feats)

    count = tok_all.shape[0] // nc
    cut, columns = nx * tok_rows, nx * (tok_rows + cot_rows)
    def term(which):
        return local_call(
            functools.partial(terms_kernel, tok_rows),
            jax.ShapeDtypeStruct((count, columns), jnp.float32),
            2 * count * columns * feats,
            2 * columns * feats,
            interpret,
            which.reshape(1),
            tok_all,
            cot_all,
            *weights,
            in_specs=[SMEM] + [VMEM] * (2 + nx),
            out_specs=VMEM,
            scratch_shapes=[pltpu.VMEM((columns, feats), jnp.bfloat16)],
        )
    other = swap(term(1 - core), "c")
    terms = term(core) + other

    share = count // nzl
    sent = terms.astype(jnp.float16).reshape(nzl, share, columns)
    got = lax.all_to_all(sent, "zl", 0, 0, tiled=True)
    proj = jnp.sum(got.astype(jnp.float32), axis=0)

    lanes = -(-2 * hid // 128) * 128
    fac = local_call(
        functools.partial(factors_kernel, nx, hid, cut),
        jax.ShapeDtypeStruct((share, nx * lanes), jnp.bfloat16),
        32 * share * nx * hid,
        8 * share * columns,
        interpret,
        proj,
        in_specs=[VMEM],
        out_specs=VMEM,
    )
    fac = lax.all_gather(fac, ("zl", "c"), axis=1, tiled=True)

    away, mine = local_call(
        functools.partial(hvp_kernel, nzl, nc),
        (
            jax.ShapeDtypeStruct((nx, 2 * hid, feats), jnp.bfloat16),
            jax.ShapeDtypeStruct((2 * hid, feats), jnp.float32),
        ),
        4 * nx * hid * nc * count * feats,
        2 * nc * count * feats,
        interpret,
        x.reshape(1),
        fac,
        tok_all,
        in_specs=[SMEM, VMEM, VMEM],
        out_specs=(VMEM, VMEM),
    )
    away = lax.all_to_all(away, "x", 0, 0, tiled=True)
    diag = jax.ShapeDtypeStruct((hid, feats), jnp.float32)
    return local_call(
        functools.partial(sum_kernel, total),
        (diag, diag),
        2 * nx * hid * feats,
        8 * nx * hid * feats,
        interpret,
        x.reshape(1),
        away,
        mine,
        gate_probe,
        up_probe,
        in_specs=[SMEM] + [VMEM] * 4,
        out_specs=(VMEM, VMEM),
    )


def solution(mesh, interpret=False):
    sizes = {**NODE, **LOCAL}
    cut = Mesh(mesh.devices.reshape(tuple(sizes.values())), tuple(sizes))
    placed = P(tuple(NODE), tuple(LOCAL))
    return jax.shard_map(
        functools.partial(on_device, interpret=interpret),
        mesh=cut,
        in_specs=(placed,) * 7,
        out_specs=(placed, placed),
        check_vma=False,
    )
```

```python
import functools

import jax
import jax.numpy as jnp
from jax import lax
from jax.experimental import pallas as pl
from jax.experimental.pallas import tpu as pltpu
from jax.sharding import Mesh, PartitionSpec as P

NODE = {"zh": 2, "x": 4, "y": 8}
LOCAL = {"zl": 4, "c": 2}

PRE_SCALE = 64.0
TAN_SCALE = 0.5
BACK_SCALE = 32.0

VMEM = pl.BlockSpec(memory_space=pltpu.VMEM)
ANY = pl.BlockSpec(memory_space=pl.ANY)
SMEM = pl.BlockSpec(memory_space=pltpu.SMEM)


def swap(value, axis):
    return lax.ppermute(value, axis, [(0, 1), (1, 0)])


def shift(value, axis, by):
    size = lax.axis_size(axis)
    return lax.ppermute(value, axis, [(i, (i + by) % size) for i in range(size)])


def mix(value, axis, by):
    return lax.ppermute(value, axis, [(i, i ^ by) for i in range(lax.axis_size(axis))])


def local_call(body, out_shape, flops, moved, interpret, *args, **options):
    return pl.pallas_call(
        body,
        out_shape=out_shape,
        cost_estimate=pl.CostEstimate(flops=flops, bytes_accessed=moved, transcendentals=0),
        compiler_params=pltpu.CompilerParams(vmem_limit_bytes=16 * 1024 * 1024),
        interpret=interpret,
        **options,
    )(*args)


def pass_kernel(value, *rest):
    pass


def after(value, others, interpret):
    return local_call(
        pass_kernel,
        jax.ShapeDtypeStruct(value.shape, value.dtype),
        0,
        0,
        interpret,
        value,
        *others,
        in_specs=[ANY] * (1 + len(others)),
        out_specs=ANY,
        input_output_aliases={0: 0},
    )


def terms_kernel(tok_rows, place, tokens, cotangents, *refs):
    *weights, out, w_all = refs
    cut = len(weights) * tok_rows
    cot_rows = weights[0].shape[0] - tok_rows
    for i, weight in enumerate(weights):
        w_all[i * tok_rows : (i + 1) * tok_rows] = weight[:tok_rows]
        start = cut + i * cot_rows
        w_all[start : start + cot_rows] = weight[tok_rows:]
    count = out.shape[0]
    half = pl.ds(pl.multiple_of(place[0] * count, count), count)
    across = (((1,), (1,)), ((), ()))
    column = lax.rem(lax.broadcasted_iota(jnp.int32, (1, cut), 1), tok_rows)
    out[:, :cut] = lax.dot_general(
        tokens[half], w_all[:cut], across, preferred_element_type=jnp.float32
    ) * jnp.where(column * 2 >= tok_rows, TAN_SCALE, PRE_SCALE)
    out[:, cut:] = BACK_SCALE * lax.dot_general(
        cotangents[half], w_all[cut:], across, preferred_element_type=jnp.float32
    )


def hvp_kernel(nzl, nc, place, fac, tokens, away, own):
    nx, width, _ = away.shape
    lanes = fac.shape[1] // (nzl * nc * nx)
    for i in range(nx):
        step = place[0] ^ i
        step = step ^ (step >> 1)
        parts = []
        for c in range(nc):
            for z in range(nzl):
                start = pl.multiple_of(((z * nc + c) * nx + step) * lanes, lanes)
                parts.append(fac[:, pl.ds(start, lanes)])
        term = lax.dot_general(
            jnp.concatenate(parts, axis=0), tokens[...], (((0,), (0,)), ((), ())),
            preferred_element_type=jnp.float32,
        )[:width]
        away[i] = term.astype(away.dtype)

        @pl.when(place[0] == i)
        def _():
            own[...] = term


def sum_kernel(total, place, away, own, gate_probe, up_probe, gate_diag, up_diag):
    both = own[...]
    for i in range(away.shape[0]):
        both += jnp.where(place[0] == i, 0.0, away[i].astype(jnp.float32))
    both = both / total
    hid = gate_diag.shape[0]
    gate_diag[...] = gate_probe[...].astype(jnp.float32) * both[:hid]
    up_diag[...] = up_probe[...].astype(jnp.float32) * both[hid:]


def factors(pre_gate, pre_up, tan_gate, tan_up, back):
    sig = jax.nn.sigmoid(pre_gate)
    slope = sig * (1.0 + pre_gate * (1.0 - sig))
    bend = sig * (1.0 - sig) * (2.0 + pre_gate * (1.0 - 2.0 * sig))
    fac_gate = (back * (tan_up * slope + pre_up * bend * tan_gate)).astype(jnp.bfloat16)
    fac_up = (back * slope * tan_gate).astype(jnp.bfloat16)
    return (fac_gate, fac_up)


def factors_kernel(nx, hid, cut, proj, out):
    tok_rows, cot_rows = cut // nx, (proj.shape[1] - cut) // nx
    lanes = out.shape[1] // nx
    for i in range(nx):
        start = i * tok_rows
        pre_gate, pre_up, tan_gate, tan_up = (
            proj[:, start + j * hid : start + (j + 1) * hid] for j in range(4)
        )
        start = cut + i * cot_rows
        fac_gate, fac_up = factors(
            pre_gate * (1.0 / PRE_SCALE),
            pre_up * (1.0 / PRE_SCALE),
            tan_gate * (1.0 / TAN_SCALE),
            tan_up * (1.0 / TAN_SCALE),
            proj[:, start : start + hid] * (1.0 / BACK_SCALE),
        )
        rest = jnp.zeros((out.shape[0], lanes - 2 * hid), jnp.bfloat16)
        out[:, i * lanes : (i + 1) * lanes] = jnp.concatenate([fac_gate, fac_up, rest], axis=1)


def stacked(parts, rows):
    row, out = 0, None
    for part in parts:
        padded = lax.pad(
            part, jnp.zeros((), part.dtype),
            ((row, rows - row - part.shape[0], 0), (0, 0, 0)),
        )
        out = padded if out is None else out + padded
        row += part.shape[0]
    return out


def on_device(
    tokens, cotangent, gate_weight, up_weight, down_weight, gate_probe, up_probe, interpret
):
    nx, ny, nzl = lax.axis_size("x"), lax.axis_size("y"), lax.axis_size("zl")
    own, feats = tokens.shape
    hid = gate_weight.shape[0]
    total = own * lax.axis_size(("zh", "x", "y"))
    nc = lax.axis_size("c")
    x, core = lax.axis_index("x"), lax.axis_index("c")

    rows = stacked([tokens, cotangent], 2 * own)
    block = jnp.stack([rows, swap(rows, "zh")], axis=0)

    tok_rows, cot_rows = 4 * hid, hid * 8 // 7
    mats = stacked(
        [gate_weight, up_weight, gate_probe, up_probe, down_weight], tok_rows + cot_rows
    )
    beside, across = mix(mats, "x", 1), mix(mats, "x", 3)

    ahead = behind = block
    blocks = [block]
    for step in range(ny // 2 - 1):
        ahead, behind = shift(ahead, "y", 1), shift(behind, "y", -1)
        if step == 0:
            behind = after(behind, [beside, across], interpret)
        if step == 1:
            beside = after(beside, [ahead], interpret)
        blocks += [ahead, behind]
    blocks += [shift(ahead[:1], "y", 1), shift(behind[1:], "y", -1)]
    weights = [mats, beside, across, mix(beside, "x", 3)]
    tok_all = jnp.concatenate([b[:, :own] for b in blocks], axis=0).reshape(-1, feats)
    cot_all = jnp.concatenate([b[:, own:] for b in blocks], axis=0).reshape(-1, feats)

    count = tok_all.shape[0] // nc
    cut, columns = nx * tok_rows, nx * (tok_rows + cot_rows)
    def term(which):
        return local_call(
            functools.partial(terms_kernel, tok_rows),
            jax.ShapeDtypeStruct((count, columns), jnp.float32),
            2 * count * columns * feats,
            2 * columns * feats,
            interpret,
            which.reshape(1),
            tok_all,
            cot_all,
            *weights,
            in_specs=[SMEM] + [VMEM] * (2 + nx),
            out_specs=VMEM,
            scratch_shapes=[pltpu.VMEM((columns, feats), jnp.bfloat16)],
        )
    other = swap(term(1 - core), "c")
    terms = term(core) + other

    share = count // nzl
    sent = terms.astype(jnp.float16).reshape(nzl, share, columns)
    got = lax.all_to_all(sent, "zl", 0, 0, tiled=True)
    proj = jnp.sum(got.astype(jnp.float32), axis=0)

    lanes = -(-2 * hid // 128) * 128
    fac = local_call(
        functools.partial(factors_kernel, nx, hid, cut),
        jax.ShapeDtypeStruct((share, nx * lanes), jnp.bfloat16),
        32 * share * nx * hid,
        8 * share * columns,
        interpret,
        proj,
        in_specs=[VMEM],
        out_specs=VMEM,
    )
    fac = lax.all_gather(fac, ("zl", "c"), axis=1, tiled=True)

    away, mine = local_call(
        functools.partial(hvp_kernel, nzl, nc),
        (
            jax.ShapeDtypeStruct((nx, 2 * hid, feats), jnp.bfloat16),
            jax.ShapeDtypeStruct((2 * hid, feats), jnp.float32),
        ),
        4 * nx * hid * nc * count * feats,
        2 * nc * count * feats,
        interpret,
        x.reshape(1),
        fac,
        tok_all,
        in_specs=[SMEM, VMEM, VMEM],
        out_specs=(VMEM, VMEM),
    )
    away = lax.all_to_all(away, "x", 0, 0, tiled=True)
    diag = jax.ShapeDtypeStruct((hid, feats), jnp.float32)
    return local_call(
        functools.partial(sum_kernel, total),
        (diag, diag),
        2 * nx * hid * feats,
        8 * nx * hid * feats,
        interpret,
        x.reshape(1),
        away,
        mine,
        gate_probe,
        up_probe,
        in_specs=[SMEM] + [VMEM] * 4,
        out_specs=(VMEM, VMEM),
    )


def solution(mesh, interpret=False):
    sizes = {**NODE, **LOCAL}
    cut = Mesh(mesh.devices.reshape(tuple(sizes.values())), tuple(sizes))
    placed = P(tuple(NODE), tuple(LOCAL))
    return jax.shard_map(
        functools.partial(on_device, interpret=interpret),
        mesh=cut,
        in_specs=(placed,) * 7,
        out_specs=(placed, placed),
        check_vma=False,
    )
```
